128 devices in a mesh: dp: 8 (over x_lo, z), tensor: 16 (over x_hi, y, core).
Axes of the slice: x: 4 (x_hi: 2, x_lo: 2; x = x_hi * 2 + x_lo), y: 4, z: 4, core: 2. Of those that a mesh axis runs over, the one named last changes fastest.
Arguments:
- inputs: bfloat16 [8, 192, 2304], P('dp'), may hold values from -6 to 6
- norm_gain: float32 [2304], replicated, may hold values from 0.1 to 1.9
- w_gate: bfloat16 [2304, 18432], P(None, 'tensor'), may hold values from -0.125 to 0.125
- w_up: bfloat16 [2304, 18432], P(None, 'tensor'), may hold values from -0.125 to 0.125
- w_down: bfloat16 [18432, 2304], P('tensor'), may hold values from -0.046875 to 0.046875
- feat_dirs: float32 [3, 8, 2304], replicated, may hold values from -6 to 6
- unit_dirs: float32 [3, 8, 18432], P(None, None, 'tensor'), may hold values from -6 to 6
- cotangent: bfloat16 [8, 192, 2304], P('dp')
- lengths: int32 [8], P('dp'), may hold values from 48 to 192, as said below
Outputs:
- mixed: bfloat16 [8, 192, 2304], P('dp')
- norm_ratio: float32 [8], P('dp')
- grad_input: bfloat16 [8, 192, 2304], P('dp', None, 'tensor')
- grad_gate: bfloat16 [2304, 18432], P('dp', 'tensor')
- grad_up: bfloat16 [2304, 18432], P('dp', 'tensor')
- grad_down: bfloat16 [18432, 2304], P('tensor', 'dp')
The draws below stay inside these ranges and needn't reach their ends.
Inputs may be any that keep to these rules, and one draw needn't show every extreme that they name: `lengths`: the first example spans all 192 positions.
All inputs are finite; a program needn't handle non-finite values.
Results may differ from the reference program's by a relative error of at most 0.025.
Values may be sent and summed in bfloat16 or wider, within the bound.
No kernel may reach another device: no remote copies, remote signals or barrier semaphores. Data moves between devices by JAX's collectives and lax.ppermute only.
A program may use at most 128 MiB of HBM per device.

```python
import math
import jax
import jax.numpy as jnp
from jax import lax

D = 2304
FF = 18432
K = 8
SEQ = 192
EX = 1
EXAMPLES = 8
N_DP = 8


def draw_cotangent(key, part):
    key = jax.random.fold_in(key, 11)
    scale_key, value_key = jax.random.split(key)
    scales = jnp.exp(jax.random.uniform(scale_key, (EXAMPLES, 1, 1), jnp.float32, math.log(0.1), math.log(10.0)))
    values = jax.random.normal(value_key, (EXAMPLES, SEQ, D), jnp.float32)
    return (values * scales).astype(jnp.bfloat16)


def draw_lengths(key, part):
    key = jax.random.fold_in(key, 23)
    drawn = jax.random.randint(key, (EXAMPLES,), SEQ // 4, SEQ + 1, jnp.int32)
    return drawn.at[0].set(SEQ)


def levels(key, shape, shards, smallest, high):
    def one(axis_at, shards_of):
        heights = jax.random.uniform(jax.random.fold_in(jax.random.fold_in(key, 6), axis_at), (shards_of,), jnp.float32, smallest / len(shards), high / len(shards))
        return jnp.repeat(jnp.exp(heights), shape[axis_at] // shards_of).reshape((-1,) + (1,) * (len(shape) - axis_at - 1))

    gain = one(*shards[0])
    for cut in shards[1:]:
        gain = gain * one(*cut)
    return gain


def normal_values(rng, extent, width, most, shards=(), kind=jnp.bfloat16):
    entries = jax.random.normal(rng, extent, jnp.float32) * width
    if len(shards) > 0:
        entries = levels(rng, extent, shards, -0.22, 0.18) * entries
    return jnp.clip(entries, min=-most, max=most).astype(kind)


def setup_inputs(seed: int = 0) -> dict:
    streams_of = jax.random.split(jax.random.key(seed), 10)
    inputs = normal_values(streams_of[0], (EXAMPLES, SEQ, D), 1.0, 6.0, ((0, 8),))
    norm_gain = jnp.clip(1.0 + 0.18 * jax.random.normal(streams_of[1], (D,), jnp.float32), 0.1, 1.9)
    w_gate = normal_values(streams_of[2], (D, FF), D ** -0.5, 0.125, ((1, 16),))
    w_up = normal_values(streams_of[3], (D, FF), D ** -0.5, 0.125, ((1, 16),))
    w_down = normal_values(streams_of[4], (FF, D), FF ** -0.5, 0.046875, ((0, 16),))
    feat_dirs = normal_values(streams_of[5], (3, K, D), 1.0, 6.0, (), jnp.float32)
    unit_dirs = normal_values(streams_of[6], (3, K, FF), 1.0, 6.0, ((2, 16),), jnp.float32)
    cotangent = draw_cotangent(jax.random.fold_in(streams_of[9], 71), 0)
    lengths = draw_lengths(jax.random.fold_in(streams_of[9], 71), 0)
    return {"inputs": inputs, "norm_gain": norm_gain, "w_gate": w_gate, "w_up": w_up, "w_down": w_down, "feat_dirs": feat_dirs, "unit_dirs": unit_dirs, "cotangent": cotangent, "lengths": lengths}


def gelu_pair(value):
    coef = math.sqrt(2.0 / math.pi)
    tangent = jnp.tanh(coef * (value + 0.044715 * value * value * value))
    activated = 0.5 * value * (1.0 + tangent)
    slope = 0.5 * (1.0 + tangent) + 0.5 * value * (1.0 - tangent * tangent) * coef * (1.0 + 3.0 * 0.044715 * value * value)
    return (activated, slope)

def reference(inputs, norm_gain, w_gate, w_up, w_down, feat_dirs, unit_dirs, cotangent, lengths):
    highest = lax.Precision.HIGHEST
    features = inputs.reshape(-1, D).astype(jnp.float32)
    inverse = lax.rsqrt(lax.optimization_barrier(jnp.mean(features * features, axis=-1, keepdims=True)) + 1e-06)
    normed = (features * inverse * norm_gain).astype(jnp.bfloat16)
    gate = jnp.dot(normed, w_gate, preferred_element_type=jnp.float32)
    up_proj = jnp.dot(normed, w_up, preferred_element_type=jnp.float32)
    activated, slope = gelu_pair(gate)
    hidden = (activated * up_proj).astype(jnp.bfloat16)
    mixed = (features + jnp.dot(hidden, w_down, preferred_element_type=jnp.float32)).astype(jnp.bfloat16)
    positions = lax.broadcasted_iota(jnp.int32, (EXAMPLES, SEQ), 1)
    mask = (positions < lengths[:, None]).astype(jnp.float32).reshape(-1, 1)
    masked_cot = cotangent.reshape(-1, D).astype(jnp.float32) * mask
    normed_wide = normed.astype(jnp.float32)
    hidden_wide = hidden.astype(jnp.float32)
    gate_coef = jnp.dot(normed_wide, feat_dirs[0].T, precision=highest)
    up_coef = jnp.dot(normed_wide, feat_dirs[1].T, precision=highest)
    down_coef = jnp.dot(hidden_wide, unit_dirs[2].T, precision=highest)
    slope_up = slope * up_proj

    def one_direction(index):
        hidden_dot = (slope_up * gate_coef[:, index][:, None] * unit_dirs[0, index][None, :] + activated * up_coef[:, index][:, None] * unit_dirs[1, index][None, :]).astype(jnp.bfloat16)
        out_dot = jnp.dot(hidden_dot, w_down, preferred_element_type=jnp.float32)
        out_dot = out_dot + down_coef[:, index][:, None] * feat_dirs[2, index][None, :]
        per_token = lax.optimization_barrier(jnp.sum(masked_cot * out_dot, axis=-1))
        return per_token.reshape(EXAMPLES, SEQ).sum(axis=1)
    loss_dot = lax.map(one_direction, jnp.arange(K, dtype=jnp.int32))
    bound = 0.5 * math.sqrt(SEQ * D * FF)
    norm_ratio = jnp.sqrt(lax.optimization_barrier(jnp.mean(loss_dot * loss_dot, axis=0))) / bound
    scale = 1.0 / (EXAMPLES * jnp.maximum(norm_ratio, 1.0))
    dout = (masked_cot.reshape(EXAMPLES, SEQ, D) * scale[:, None, None]).reshape(-1, D).astype(jnp.bfloat16)
    dhidden = jnp.dot(dout, w_down.T, preferred_element_type=jnp.float32)
    dgate = (dhidden * up_proj * slope).astype(jnp.bfloat16)
    dup = (dhidden * activated).astype(jnp.bfloat16)
    block_rows = EX * SEQ

    def add_block(totals, block):
        start = (block * block_rows).astype(jnp.int32)
        normed_block = lax.dynamic_slice_in_dim(normed, start, block_rows, 0)
        hidden_block = lax.dynamic_slice_in_dim(hidden, start, block_rows, 0)
        dgate_block = lax.dynamic_slice_in_dim(dgate, start, block_rows, 0)
        dup_block = lax.dynamic_slice_in_dim(dup, start, block_rows, 0)
        dout_block = lax.dynamic_slice_in_dim(dout, start, block_rows, 0)
        part_gate = jnp.dot(normed_block.T, dgate_block, preferred_element_type=jnp.float32)
        part_up = jnp.dot(normed_block.T, dup_block, preferred_element_type=jnp.float32)
        part_down = jnp.dot(hidden_block.T, dout_block, preferred_element_type=jnp.float32)
        part_gate = part_gate.astype(jnp.bfloat16).astype(jnp.float32)
        part_up = part_up.astype(jnp.bfloat16).astype(jnp.float32)
        part_down = part_down.astype(jnp.bfloat16).astype(jnp.float32)
        return ((totals[0] + part_gate, totals[1] + part_up, totals[2] + part_down), None)
    start_totals = (jnp.zeros((D, FF), jnp.float32), jnp.zeros((D, FF), jnp.float32), jnp.zeros((FF, D), jnp.float32))
    totals, _ = lax.scan(add_block, start_totals, jnp.arange(N_DP, dtype=jnp.int32))
    dnormed = jnp.dot(dgate, w_gate.T, preferred_element_type=jnp.float32) + jnp.dot(dup, w_up.T, preferred_element_type=jnp.float32)
    gained = dnormed * norm_gain
    back = gained * inverse - features * inverse * inverse * inverse * lax.optimization_barrier(jnp.mean(gained * features, axis=-1, keepdims=True))
    grad_input = (dout.astype(jnp.float32) + back).astype(jnp.bfloat16).reshape(EXAMPLES, SEQ, D)
    return (mixed.reshape(EXAMPLES, SEQ, D), norm_ratio, grad_input, totals[0].astype(jnp.bfloat16), totals[1].astype(jnp.bfloat16), totals[2].astype(jnp.bfloat16))
```

```python
import math

import jax
import jax.numpy as jnp
from jax import lax
from jax.sharding import PartitionSpec as P

D = 2304
FF = 18432
SEQ = 192
K = 8
N_DP = 8
N_T = 16
UNITS = FF // N_T
SLICE = D // N_DP
OWN = D // N_T
BOTH = ("dp", "tensor")


def device_index(x, y, z, core):
    x, y, z = x % 4, y % 4, z % 4
    return ((x % 2) * 4 + z) * N_T + ((x // 2) * 4 + y) * 2 + core


def move(array, target):
    pairs = [
        (device_index(x, y, z, core), device_index(*target(x, y, z, core)))
        for x in range(4)
        for y in range(4)
        for z in range(4)
        for core in range(2)
    ]
    return lax.ppermute(array, BOTH, pairs)


def to_pair(x, y, z, core):
    return (x ^ 1, y, z, core)


def to_up(x, y, z, core):
    return (x, y, z + 1, core)


def to_down(x, y, z, core):
    return (x, y, z - 1, core)


def to_sibling(x, y, z, core):
    return (x, y, z, 1 - core)


def to_far(x, y, z, core):
    return (x ^ 2, y, z, core)


def along_y(step):
    return lambda x, y, z, core: (x, y + step, z, core)


def along_z(step):
    return lambda x, y, z, core: (x, y, z + step, core)


def gelu_pair(value):
    coef = math.sqrt(2.0 / math.pi)
    tangent = jnp.tanh(coef * (value + 0.044715 * value * value * value))
    activated = 0.5 * value * (1.0 + tangent)
    slope = 0.5 * (1.0 + tangent) + 0.5 * value * (1.0 - tangent * tangent) * coef * (
        1.0 + 3.0 * 0.044715 * value * value
    )
    return (activated, slope)


def contract_last(left, right):
    return lax.dot_general(
        left, right, (((1,), (1,)), ((), ())), preferred_element_type=jnp.float32
    )


def contract_first(left, right):
    return lax.dot_general(
        left, right, (((0,), (0,)), ((), ())), preferred_element_type=jnp.float32
    )


def unit_work(normed, cot, w_gate, w_up, w_down):
    gate = jnp.dot(normed, w_gate, preferred_element_type=jnp.float32)
    up_proj = jnp.dot(normed, w_up, preferred_element_type=jnp.float32)
    dhidden = contract_last(cot, w_down)
    activated, slope = gelu_pair(gate)
    hidden = (activated * up_proj).astype(jnp.bfloat16)
    dgate = (dhidden * up_proj * slope).astype(jnp.bfloat16)
    dup = (dhidden * activated).astype(jnp.bfloat16)
    return hidden, dgate, dup


def pick(array, index):
    return lax.dynamic_index_in_dim(array, index, 0, keepdims=False)


def split_wide(value):
    high = value.astype(jnp.bfloat16)
    return high, (value - high.astype(jnp.float32)).astype(jnp.bfloat16)


def shards(inputs, norm_gain, w_gate, w_up, w_down, feat_dirs, unit_dirs, cotangent, lengths):
    highest = lax.Precision.HIGHEST
    t_index = lax.axis_index("tensor")
    d_index = lax.axis_index("dp")
    core = t_index % 2
    y_at = (t_index // 2) % 4
    x_high = t_index // 8
    features = inputs.reshape(SEQ, D).astype(jnp.float32)
    inverse = lax.rsqrt(jnp.mean(features * features, axis=-1, keepdims=True) + 1e-06)
    normed = (features * inverse * norm_gain).astype(jnp.bfloat16)
    positions = lax.broadcasted_iota(jnp.int32, (SEQ, 1), 0)
    mask = (positions < lengths[:, None]).astype(jnp.float32)
    masked_wide = cotangent.reshape(SEQ, D).astype(jnp.float32) * mask
    masked = masked_wide.astype(jnp.bfloat16)

    mine = jnp.stack(
        [pick(normed.reshape(2, 2, 48, D), core), pick(masked.reshape(2, 2, 48, D), core)], axis=1
    )
    from_pair = move(mine, to_pair)
    from_down = move(mine, to_up)
    from_up = move(mine, to_down)

    hidden, dgate, dup = unit_work(normed, masked, w_gate, w_up, w_down)
    branch = jnp.dot(hidden, w_down, preferred_element_type=jnp.float32)
    dnormed = contract_last(dgate, w_gate) + contract_last(dup, w_up)

    gate_coef = jnp.dot(normed.astype(jnp.float32), feat_dirs[0].T, precision=highest)
    up_coef = jnp.dot(normed.astype(jnp.float32), feat_dirs[1].T, precision=highest)
    cot_coef = jnp.dot(masked_wide, feat_dirs[2].T, precision=highest)
    pieces = []
    for array, coef, dirs in (
        (dgate, gate_coef, unit_dirs[0]),
        (dup, up_coef, unit_dirs[1]),
        (hidden, cot_coef, unit_dirs[2]),
    ):
        high, low = split_wide(dirs)
        onto = contract_last(array, high) + contract_last(array, low)
        pieces.append(jnp.sum(onto * coef, axis=0))
    loss_dot = (pieces[0] + pieces[1] + pieces[2])[None, :]

    gained = dnormed * norm_gain
    back = gained * inverse - features * inverse * inverse * inverse * jnp.mean(
        gained * features, axis=-1, keepdims=True
    )

    both = jnp.stack([branch, back]).astype(jnp.bfloat16)
    both = both.reshape(2, SEQ, 2, 4, 2, OWN).transpose(4, 3, 2, 0, 1, 5)
    kept = pick(both, core).astype(jnp.float32) + move(pick(both, 1 - core), to_sibling).astype(
        jnp.float32
    )
    loss_dot = loss_dot + move(loss_dot, to_sibling)
    kept = kept.astype(jnp.bfloat16)
    total = pick(kept, y_at).astype(jnp.float32)
    loss_sum = loss_dot
    for step in (1, 2, 3):
        total = total + move(pick(kept, (y_at + step) % 4), along_y(step)).astype(jnp.float32)
        loss_sum = loss_sum + move(loss_dot, along_y(step))
    total = total.astype(jnp.bfloat16)
    total = pick(total, x_high).astype(jnp.float32) + move(
        pick(total, 1 - x_high), to_far
    ).astype(jnp.float32)
    loss_dot = loss_sum + move(loss_sum, to_far)

    bound = 0.5 * math.sqrt(SEQ * D * FF)
    norm_ratio = jnp.sqrt(jnp.mean(loss_dot * loss_dot, axis=1)) / bound
    scale = 1.0 / (N_DP * jnp.maximum(norm_ratio, 1.0))

    column = total[0].astype(jnp.bfloat16)
    other = move(column, to_far)
    pair = jnp.where(x_high == 0, jnp.stack([column, other]), jnp.stack([other, column]))
    rolled = jnp.stack([pair] + [move(pair, along_y(-step)) for step in (1, 2, 3)])
    quad = jnp.roll(rolled, y_at, axis=0)
    sibling = move(quad, to_sibling)
    every = jnp.where(core == 0, jnp.stack([quad, sibling]), jnp.stack([sibling, quad]))
    branch_total = every.transpose(3, 2, 1, 0, 4).reshape(SEQ, D).astype(jnp.float32)
    mixed = (features + branch_total).astype(jnp.bfloat16).reshape(1, SEQ, D)

    own_cot = lax.dynamic_slice_in_dim(masked, t_index * OWN, OWN, 1).astype(jnp.float32)
    grad_input = ((total[1] + own_cot) * scale).astype(jnp.bfloat16).reshape(1, SEQ, OWN)

    scale_row = jnp.broadcast_to(scale[None, :], (1, 128))
    pair_row = move(scale_row, to_pair)
    two = jnp.concatenate([scale_row, pair_row], axis=0)
    two_down = move(two, along_z(1))
    two_up = move(two, along_z(-1))
    two_far = move(two, along_z(2))

    x_second = move(jnp.stack([from_down[0], from_up[0]]), to_pair)
    up_second = move(jnp.stack([from_pair[1], from_down[0]]), to_up)
    down_second = move(jnp.stack([from_pair[1], from_up[1]]), to_down)
    up_third = move(x_second[0], to_up)
    down_third = move(down_second[0], to_down)

    def with_sibling(array):
        array = array.reshape(-1, 2, 48, D)
        return jnp.concatenate([array, move(array, to_sibling)])

    first = [with_sibling(a) for a in (from_pair, from_down, from_up)]
    second = [with_sibling(a) for a in (x_second, up_second, down_second)]
    third = [with_sibling(a) for a in (up_third, down_third)]

    def rows(parts, which):
        return jnp.concatenate([p[:, which].reshape(-1, D) for p in parts])

    def factor(two_rows, place, count):
        return jnp.full((count, 1), two_rows[place, 0], jnp.float32)

    n48 = 48
    scales_first = [
        factor(two, 1, 4 * n48),
        factor(two_down, 0, 4 * n48),
        factor(two_up, 0, 4 * n48),
    ]
    scales_second = [
        factor(two_down, 1, n48), factor(two_up, 1, n48),
        factor(two_down, 1, n48), factor(two_up, 1, n48),
        factor(two_down, 1, n48), factor(two_far, 0, n48),
        factor(two_down, 1, n48), factor(two_far, 0, n48),
        factor(two_up, 1, n48), factor(two_far, 0, n48),
        factor(two_up, 1, n48), factor(two_far, 0, n48),
    ]
    scales_third = [factor(two_far, 1, 4 * n48)]

    groups = [((normed, masked), (hidden, dgate, dup), factor(two, 0, SEQ))]
    for parts, factors in ((first, scales_first), (second, scales_second), (third, scales_third)):
        group = (rows(parts, 0), rows(parts, 1))
        groups.append(
            (group, unit_work(*group, w_gate, w_up, w_down), jnp.concatenate(factors))
        )
    part_gate = part_up = part_down = 0.0
    for (group_normed, group_cot), (g_hidden, g_dgate, g_dup), factors in groups:
        wide = lax.dynamic_slice_in_dim(group_normed, d_index * SLICE, SLICE, 1)
        left = (wide.astype(jnp.float32) * factors).astype(jnp.bfloat16)
        wide = lax.dynamic_slice_in_dim(group_cot, d_index * SLICE, SLICE, 1)
        right = (wide.astype(jnp.float32) * factors).astype(jnp.bfloat16)
        part_gate += contract_first(left, g_dgate)
        part_up += contract_first(left, g_dup)
        part_down += contract_first(g_hidden, right)
    return (
        mixed,
        norm_ratio,
        grad_input,
        part_gate.astype(jnp.bfloat16),
        part_up.astype(jnp.bfloat16),
        part_down.astype(jnp.bfloat16),
    )


def solution(mesh):
    placed = (
        P("dp", None, None),
        P(),
        P(None, "tensor"),
        P(None, "tensor"),
        P("tensor", None),
        P(),
        P(None, None, "tensor"),
        P("dp", None, None),
        P("dp"),
    )
    return jax.shard_map(
        shards,
        mesh=mesh,
        in_specs=placed,
        out_specs=(
            P("dp", None, None),
            P("dp"),
            P("dp", None, "tensor"),
            P("dp", "tensor"),
            P("dp", "tensor"),
            P("tensor", "dp"),
        ),
        check_vma=False,
    )
```

```python
import functools
import math

import jax
import jax.numpy as jnp
from jax import lax
from jax.experimental import pallas as pl
from jax.experimental.pallas import tpu as pltpu
from jax.sharding import PartitionSpec as P

D = 2304
FF = 18432
SEQ = 192
K = 8
N_DP = 8
N_T = 16
UNITS = FF // N_T
SLICE = D // N_DP
OWN = D // N_T
BOTH = ("dp", "tensor")
TILE = 384
WINDOW = 384


def device_index(x, y, z, core):
    x, y, z = x % 4, y % 4, z % 4
    return ((x % 2) * 4 + z) * N_T + ((x // 2) * 4 + y) * 2 + core


def move(array, target):
    pairs = [
        (device_index(x, y, z, core), device_index(*target(x, y, z, core)))
        for x in range(4)
        for y in range(4)
        for z in range(4)
        for core in range(2)
    ]
    return lax.ppermute(array, BOTH, pairs)


def to_pair(x, y, z, core):
    return (x ^ 1, y, z, core)


def to_up(x, y, z, core):
    return (x, y, z + 1, core)


def to_down(x, y, z, core):
    return (x, y, z - 1, core)


def to_sibling(x, y, z, core):
    return (x, y, z, 1 - core)


def to_far(x, y, z, core):
    return (x ^ 2, y, z, core)


def along_y(step):
    return lambda x, y, z, core: (x, y + step, z, core)


def along_z(step):
    return lambda x, y, z, core: (x, y, z + step, core)


def gelu_pair(value):
    coef = math.sqrt(2.0 / math.pi)
    tangent = jnp.tanh(coef * (value + 0.044715 * value * value * value))
    activated = 0.5 * value * (1.0 + tangent)
    slope = 0.5 * (1.0 + tangent) + 0.5 * value * (1.0 - tangent * tangent) * coef * (
        1.0 + 3.0 * 0.044715 * value * value
    )
    return (activated, slope)


def contract_last(left, right):
    return lax.dot_general(
        left, right, (((1,), (1,)), ((), ())), preferred_element_type=jnp.float32
    )


def contract_first(left, right):
    return lax.dot_general(
        left, right, (((0,), (0,)), ((), ())), preferred_element_type=jnp.float32
    )


def own_kernel(
    start_ref, core_ref, normed, masked, inputs, inverse, gain, gate_w, up_w, down_w, feats, units,
    hidden, dgate, dup, kept, sent, normed_cut, cot_cut, branch, dnormed, onto,
):
    step = pl.program_id(0)

    @pl.when(step == 0)
    def _():
        branch[...] = jnp.zeros_like(branch)
        dnormed[...] = jnp.zeros_like(dnormed)
        onto[...] = jnp.zeros_like(onto)
        window = pl.ds(pl.multiple_of(start_ref[0], 128), WINDOW)
        normed_cut[...] = normed[:, window]
        cot_cut[...] = masked[:, window]

    def split_dirs(dirs):
        high = dirs.astype(jnp.bfloat16).astype(jnp.float32)
        return jnp.concatenate([high, dirs - high]).astype(jnp.bfloat16)

    gate = jnp.dot(normed[...], gate_w[...], preferred_element_type=jnp.float32)
    up_proj = jnp.dot(normed[...], up_w[...], preferred_element_type=jnp.float32)
    dhidden = contract_last(masked[...], down_w[...])
    activated, slope = gelu_pair(gate)
    hidden[...] = (activated * up_proj).astype(jnp.bfloat16)
    dgate[...] = (dhidden * up_proj * slope).astype(jnp.bfloat16)
    dup[...] = (dhidden * activated).astype(jnp.bfloat16)
    branch[...] += jnp.dot(hidden[...], down_w[...], preferred_element_type=jnp.float32)
    dnormed[...] += contract_last(dgate[...], gate_w[...]) + contract_last(dup[...], up_w[...])
    for at, array in enumerate((dgate, dup, hidden)):
        onto[at] += contract_last(array[...], split_dirs(units[at]))

    @pl.when(step == pl.num_programs(0) - 1)
    def _():
        loss = jnp.zeros((1, K), jnp.float32)
        for at, array in enumerate((normed, normed, masked)):
            coef = contract_last(array[...], split_dirs(feats[at]))
            both = onto[at]
            loss += jnp.sum(
                (coef[:, :K] + coef[:, K:]) * (both[:, :K] + both[:, K:]), axis=0, keepdims=True
            )
        wide = inputs[...].astype(jnp.float32)
        inv = inverse[...]
        gained = dnormed[...] * gain[...]
        back = gained * inv - wide * (inv * inv * inv) * jnp.mean(
            gained * wide, axis=-1, keepdims=True
        )
        branch_t = branch[...].T.astype(jnp.bfloat16)
        back_t = back.T.astype(jnp.bfloat16)
        loss_rows = jnp.broadcast_to(loss, (16, K)).astype(jnp.bfloat16)
        first_core = core_ref[0] == 0
        for place in range(8):
            t = place % 2 * 8 + place // 2 * 2
            for into, low_first in ((kept, first_core), (sent, jnp.logical_not(first_core))):
                for at, array in enumerate((back_t, branch_t)):
                    into[place, at * OWN : (at + 1) * OWN, :] = jnp.where(
                        low_first,
                        array[t * OWN : (t + 1) * OWN],
                        array[(t + 1) * OWN : (t + 2) * OWN],
                    )
                into[place, 2 * OWN :, :] = jnp.zeros((16, SEQ), jnp.bfloat16)
                into[place, 2 * OWN :, :K] = loss_rows


def own_work(start, core, normed, masked, inputs, inverse, gain, w_gate, w_up, w_down, feats, units):
    def whole(*shape):
        return pl.BlockSpec(shape, lambda u: (0,) * len(shape))

    by_unit = pl.BlockSpec((SEQ, TILE), lambda u: (0, u))
    return pl.pallas_call(
        own_kernel,
        grid=(UNITS // TILE,),
        in_specs=[
            pl.BlockSpec(memory_space=pltpu.SMEM),
            pl.BlockSpec(memory_space=pltpu.SMEM),
            whole(SEQ, D), whole(SEQ, D), whole(SEQ, D), whole(SEQ, 1), whole(1, D),
            pl.BlockSpec((D, TILE), lambda u: (0, u)),
            pl.BlockSpec((D, TILE), lambda u: (0, u)),
            pl.BlockSpec((TILE, D), lambda u: (u, 0)),
            whole(3, K, D),
            pl.BlockSpec((3, K, TILE), lambda u: (0, 0, u)),
        ],
        out_specs=[by_unit] * 3
        + [whole(8, 2 * OWN + 16, SEQ)] * 2
        + [whole(SEQ, WINDOW), whole(SEQ, WINDOW)],
        out_shape=[jax.ShapeDtypeStruct((SEQ, UNITS), jnp.bfloat16)] * 3
        + [jax.ShapeDtypeStruct((8, 2 * OWN + 16, SEQ), jnp.bfloat16)] * 2
        + [jax.ShapeDtypeStruct((SEQ, WINDOW), jnp.bfloat16)] * 2,
        scratch_shapes=[
            pltpu.VMEM((SEQ, D), jnp.float32),
            pltpu.VMEM((SEQ, D), jnp.float32),
            pltpu.VMEM((3, SEQ, 2 * K), jnp.float32),
        ],
        compiler_params=pltpu.CompilerParams(vmem_limit_bytes=58 * 2**20),
        cost_estimate=pl.CostEstimate(
            flops=10 * SEQ * D * UNITS, bytes_accessed=7 * D * UNITS, transcendentals=SEQ * UNITS
        ),
    )(start, core, normed, masked, inputs, inverse, gain, w_gate, w_up, w_down, feats, units)


def collect_kernel(pieces, count, start_ref, *refs):
    sources, (normed, cot, normed_cut, cot_cut, sems) = refs[:count], refs[count:]
    window = pl.ds(pl.multiple_of(start_ref[0], 128), WINDOW)
    copies = []
    row = 0
    for at, (src, item, size) in enumerate(pieces):
        for which, into in enumerate((normed, cot)):
            copies.append(
                pltpu.make_async_copy(
                    sources[src].at[item, which],
                    into.at[pl.ds(row, size)],
                    sems.at[2 * at + which],
                )
            )
        row += size
    for copy in copies:
        copy.start()
    for copy in copies:
        copy.wait()
    normed_cut[...] = normed[:, window]
    cot_cut[...] = cot[:, window]


def collect(start, sources, pieces):
    rows = sum(piece[2] for piece in pieces)
    return pl.pallas_call(
        functools.partial(collect_kernel, pieces, len(sources)),
        in_specs=[pl.BlockSpec(memory_space=pltpu.SMEM)]
        + [pl.BlockSpec(memory_space=pl.ANY)] * len(sources),
        out_shape=[jax.ShapeDtypeStruct((rows, D), jnp.bfloat16)] * 2
        + [jax.ShapeDtypeStruct((rows, WINDOW), jnp.bfloat16)] * 2,
        scratch_shapes=[pltpu.SemaphoreType.DMA((2 * len(pieces),))],
        compiler_params=pltpu.CompilerParams(vmem_limit_bytes=16 * 2**20),
        cost_estimate=pl.CostEstimate(
            flops=0, bytes_accessed=10 * rows * D, transcendentals=0
        ),
    )(start, *sources)


def unit_work(normed, cot, w_gate, w_up, w_down):
    gate = jnp.dot(normed, w_gate, preferred_element_type=jnp.float32)
    up_proj = jnp.dot(normed, w_up, preferred_element_type=jnp.float32)
    dhidden = contract_last(cot, w_down)
    activated, slope = gelu_pair(gate)
    hidden = (activated * up_proj).astype(jnp.bfloat16)
    dgate = (dhidden * up_proj * slope).astype(jnp.bfloat16)
    dup = (dhidden * activated).astype(jnp.bfloat16)
    return hidden, dgate, dup


def grad_kernel(owners, sizes, offset_ref, scale_ref, *refs):
    groups, refs = refs[: 5 * len(sizes)], refs[5 * len(sizes) :]
    out_gate, out_up, out_down, left, right, wide_gate, wide_up = refs

    @pl.when(pl.program_id(0) == 0)
    def _():
        row = 0
        for at in range(len(sizes)):
            inside = 0
            for owner, size in owners[at]:
                scale = scale_ref[owner]
                here, there = pl.ds(inside, size), pl.ds(row, size)
                left[there, :] = (groups[5 * at + 3][here, :].astype(jnp.float32) * scale).astype(
                    jnp.bfloat16
                )
                right[there, :] = (
                    groups[5 * at + 4][here, :].astype(jnp.float32) * scale
                ).astype(jnp.bfloat16)
                inside += size
                row += size

    gate_sum = up_sum = down_sum = None
    row = 0
    for at, size in enumerate(sizes):
        hidden, dgate, dup = groups[5 * at : 5 * at + 3]
        these = pl.ds(row, size)
        row += size
        terms = (
            contract_first(left[these, :], dgate[...]),
            contract_first(left[these, :], dup[...]),
            contract_first(hidden[...], right[these, :]),
        )
        if gate_sum is None:
            gate_sum, up_sum, down_sum = terms
        else:
            gate_sum, up_sum, down_sum = gate_sum + terms[0], up_sum + terms[1], down_sum + terms[2]
    offset = pl.multiple_of(offset_ref[0], 32)
    wide_gate[...] = gate_sum
    wide_up[...] = up_sum
    out_gate[...] = wide_gate[pl.ds(offset, SLICE), :].astype(jnp.bfloat16)
    out_up[...] = wide_up[pl.ds(offset, SLICE), :].astype(jnp.bfloat16)
    out_down[...] = pltpu.roll(down_sum, WINDOW - offset, 1)[:, :SLICE].astype(jnp.bfloat16)


def grad_work(offset, scales, groups, owners):
    sizes = [group[0].shape[0] for group in groups]
    rows = sum(sizes)
    specs = []
    for size in sizes:
        by_unit = pl.BlockSpec((size, TILE), lambda u: (0, u))
        whole = pl.BlockSpec((size, WINDOW), lambda u: (0, 0))
        specs += [by_unit] * 3 + [whole] * 2
    return pl.pallas_call(
        functools.partial(grad_kernel, owners, sizes),
        grid=(UNITS // TILE,),
        in_specs=[pl.BlockSpec(memory_space=pltpu.SMEM)] * 2 + specs,
        out_specs=[
            pl.BlockSpec((SLICE, TILE), lambda u: (0, u)),
            pl.BlockSpec((SLICE, TILE), lambda u: (0, u)),
            pl.BlockSpec((TILE, SLICE), lambda u: (u, 0)),
        ],
        out_shape=[
            jax.ShapeDtypeStruct((SLICE, UNITS), jnp.bfloat16),
            jax.ShapeDtypeStruct((SLICE, UNITS), jnp.bfloat16),
            jax.ShapeDtypeStruct((UNITS, SLICE), jnp.bfloat16),
        ],
        scratch_shapes=[
            pltpu.VMEM((rows, WINDOW), jnp.bfloat16),
            pltpu.VMEM((rows, WINDOW), jnp.bfloat16),
            pltpu.VMEM((WINDOW, TILE), jnp.float32),
            pltpu.VMEM((WINDOW, TILE), jnp.float32),
        ],
        compiler_params=pltpu.CompilerParams(vmem_limit_bytes=58 * 2**20),
        cost_estimate=pl.CostEstimate(
            flops=6 * rows * WINDOW * UNITS,
            bytes_accessed=6 * rows * UNITS + 6 * SLICE * UNITS + 4 * rows * WINDOW,
            transcendentals=0,
        ),
    )(offset, scales, *[array for group in groups for array in group])


def pick(array, index):
    return lax.dynamic_index_in_dim(array, index, 0, keepdims=False)


def after(arrays, *earlier):
    return lax.optimization_barrier((arrays, earlier))[0]


def mix_kernel(y_ref, core_ref, inputs, *refs):
    pieces, mixed, total = refs[:8], refs[8], refs[9]
    for side in range(2):
        for step in range(4):
            piece = pieces[4 * side + step]
            y_at = lax.rem(y_ref[0] + step, 4)
            core = core_ref[0] if side == 0 else 1 - core_ref[0]
            for x_high in range(2):
                row = (x_high * 8 + y_at * 2 + core) * OWN
                total[pl.ds(pl.multiple_of(row, 16), OWN), :] = piece[x_high, :OWN, :].astype(
                    jnp.float32
                )
    mixed[...] = (inputs[...].astype(jnp.float32) + total[...].T).astype(jnp.bfloat16)


def mix(y_at, core, inputs, pieces):
    smem = pl.BlockSpec(memory_space=pltpu.SMEM)
    vmem = pl.BlockSpec(memory_space=pltpu.VMEM)
    return pl.pallas_call(
        mix_kernel,
        in_specs=[smem, smem] + [vmem] * 9,
        out_shape=jax.ShapeDtypeStruct((SEQ, D), jnp.bfloat16),
        scratch_shapes=[pltpu.VMEM((D, SEQ), jnp.float32)],
        compiler_params=pltpu.CompilerParams(vmem_limit_bytes=24 * 2**20),
    )(y_at, core, inputs, *pieces)


def shards(inputs, norm_gain, w_gate, w_up, w_down, feat_dirs, unit_dirs, cotangent, lengths):
    t_index = lax.axis_index("tensor")
    d_index = lax.axis_index("dp")
    core = t_index % 2
    y_at = (t_index // 2) % 4
    x_high = t_index // 8
    features = inputs.reshape(SEQ, D).astype(jnp.float32)
    inverse = lax.rsqrt(jnp.mean(features * features, axis=-1, keepdims=True) + 1e-06)
    normed = (features * inverse * norm_gain).astype(jnp.bfloat16)
    positions = lax.broadcasted_iota(jnp.int32, (SEQ, 1), 0)
    mask = (positions < lengths[:, None]).astype(jnp.float32)
    masked_wide = cotangent.reshape(SEQ, D).astype(jnp.float32) * mask
    masked = masked_wide.astype(jnp.bfloat16)

    mine = jnp.stack(
        [pick(normed.reshape(2, 2, 48, D), core), pick(masked.reshape(2, 2, 48, D), core)], axis=1
    )
    from_pair = move(mine, to_pair)
    from_down = move(mine, to_up)
    from_up = move(mine, to_down)

    first_column = d_index * SLICE
    window_start = (first_column // 128 * 128).astype(jnp.int32)[None]
    window_offset = (first_column % 128).astype(jnp.int32)[None]
    core_index = core.astype(jnp.int32)[None]
    *own, kept, sent, own_normed_cut, own_cot_cut = own_work(
        window_start, core_index, normed, masked, inputs.reshape(SEQ, D), inverse,
        norm_gain[None, :], w_gate, w_up, w_down, feat_dirs, unit_dirs,
    )
    own = (*own, own_normed_cut, own_cot_cut)

    from_pair, from_down, from_up, kept = after((from_pair, from_down, from_up, kept), sent)
    kept_sibling = move(sent, to_sibling)
    x_second = move(from_down, to_pair)
    up_second = move(from_down, to_up)
    down_second = move(from_pair, to_down)
    first_sources = [(a, move(a, to_sibling)) for a in (from_pair, from_down, from_up)]
    kept = kept.astype(jnp.float32) + kept_sibling.astype(jnp.float32)
    kept = kept.astype(jnp.bfloat16).reshape(4, 2, 2 * OWN + 16, SEQ)
    arrived = [move(pick(kept, (y_at + step) % 4), along_y(step)) for step in (1, 2, 3)]
    total = pick(kept, y_at)

    def group_of(sources, owners):
        pieces = []
        flat = []
        for at, (pair, owner) in enumerate(zip(sources, owners)):
            for which in range(2):
                for item in range(pair[0].shape[0]):
                    pieces.append((2 * at + which, item, 48))
                    flat.append((owner, 48))
        arrays = [a for pair in sources for a in pair]
        g_normed, g_cot, normed_cut, cot_cut = collect(window_start, arrays, tuple(pieces))
        worked = unit_work(g_normed, g_cot, w_gate, w_up, w_down)
        return (*worked, normed_cut, cot_cut), tuple(flat)

    first_sources = after(first_sources, total)
    first, owners_first = group_of(first_sources, (1, 2, 4))

    arrived, total, x_second, up_second, down_second = after(
        (arrived, total, x_second, up_second, down_second), first
    )
    third = [move(x_second[:1], to_up), move(down_second[1:], to_down)]
    second_sources = [(a, move(a, to_sibling)) for a in (x_second, up_second, down_second)]
    total = sum((a.astype(jnp.float32) for a in arrived), total.astype(jnp.float32))
    total = total.astype(jnp.bfloat16)
    total_far = move(total, to_far)

    second, owners_second = group_of(second_sources, (3, 6, 5))

    total, total_far, third = after((total, total_far, third), second)
    third_sources = [(a, move(a, to_sibling)) for a in third]
    total = total.astype(jnp.float32) + total_far.astype(jnp.float32)
    loss_dot = total[:1, 2 * OWN, :K]
    bound = 0.5 * math.sqrt(SEQ * D * FF)
    own_ratio = jnp.sqrt(jnp.mean(loss_dot * loss_dot, axis=1)) / bound
    scale = 1.0 / (N_DP * jnp.maximum(own_ratio, 1.0))
    scale_row = jnp.broadcast_to(scale[None, :], (1, 128))
    scale_pair = move(scale_row, to_pair)
    branch = total[:, OWN:].astype(jnp.bfloat16)
    branches = [branch] + [move(branch, along_y(-step)) for step in (1, 2, 3)]

    third, owners_third = group_of(third_sources, (7, 7))

    scale_pair, branches = after((scale_pair, branches), third)
    two = jnp.concatenate([scale_row, scale_pair], axis=0)
    two_down = move(two, along_z(1))
    two_up = move(two, along_z(-1))
    two_far = move(two, along_z(2))
    siblings = [move(a, to_sibling) for a in branches]
    own_cot = lax.dynamic_slice_in_dim(masked, t_index * OWN, OWN, 1).astype(jnp.float32)
    own_back = pick(total, x_high)[:OWN]
    grad_input = ((own_back.T + own_cot) * scale).astype(jnp.bfloat16).reshape(1, SEQ, OWN)

    scales = jnp.concatenate([two[:, 0], two_down[:, 0], two_up[:, 0], two_far[:, 0]])
    grads = grad_work(
        window_offset,
        scales,
        (own, first, second, third),
        (((0, SEQ),), owners_first, owners_second, owners_third),
    )
    branches, siblings = after((branches, siblings), grads)
    mixed = mix(
        y_at.astype(jnp.int32)[None], core_index, inputs.reshape(SEQ, D), branches + siblings
    ).reshape(1, SEQ, D)
    every_loss = jnp.stack([a[0, OWN, :K] for a in branches + siblings])
    shared_loss = pick(every_loss, (4 - y_at) % 4 + 4 * core).astype(jnp.float32)[None, :]
    norm_ratio = jnp.sqrt(jnp.mean(shared_loss * shared_loss, axis=1)) / bound
    return (mixed, norm_ratio, grad_input, *grads)


def solution(mesh):
    placed = (
        P("dp", None, None),
        P(),
        P(None, "tensor"),
        P(None, "tensor"),
        P("tensor", None),
        P(),
        P(None, None, "tensor"),
        P("dp", None, None),
        P("dp"),
    )
    return jax.shard_map(
        shards,
        mesh=mesh,
        in_specs=placed,
        out_specs=(
            P("dp", None, None),
            P("dp"),
            P("dp", None, "tensor"),
            P("dp", "tensor"),
            P("dp", "tensor"),
            P("tensor", "dp"),
        ),
        check_vma=False,
    )
```

```python
import functools
import math

import jax
import jax.numpy as jnp
from jax import lax
from jax.experimental import pallas as pl
from jax.experimental.pallas import tpu as pltpu
from jax.sharding import PartitionSpec as P

D = 2304
FF = 18432
SEQ = 192
K = 8
N_DP = 8
N_T = 16
UNITS = FF // N_T
SLICE = D // N_DP
OWN = D // N_T
BOTH = ("dp", "tensor")
TILE = 384
WINDOW = 384
LANES = 256
ROWS = 2 * OWN + 16


def device_index(x, y, z, core):
    x, y, z = x % 4, y % 4, z % 4
    return ((x % 2) * 4 + z) * N_T + ((x // 2) * 4 + y) * 2 + core


def move(array, target):
    pairs = [
        (device_index(x, y, z, core), device_index(*target(x, y, z, core)))
        for x in range(4)
        for y in range(4)
        for z in range(4)
        for core in range(2)
    ]
    return lax.ppermute(array, BOTH, pairs)


def to_pair(x, y, z, core):
    return (x ^ 1, y, z, core)


def to_up(x, y, z, core):
    return (x, y, z + 1, core)


def to_down(x, y, z, core):
    return (x, y, z - 1, core)


def to_sibling(x, y, z, core):
    return (x, y, z, 1 - core)


def to_far(x, y, z, core):
    return (x ^ 2, y, z, core)


def along_y(step):
    return lambda x, y, z, core: (x, y + step, z, core)


def along_z(step):
    return lambda x, y, z, core: (x, y, z + step, core)


def gelu_pair(value):
    coef = math.sqrt(2.0 / math.pi)
    tangent = jnp.tanh(coef * (value + 0.044715 * value * value * value))
    activated = 0.5 * value * (1.0 + tangent)
    slope = 0.5 * (1.0 + tangent) + 0.5 * value * (1.0 - tangent * tangent) * coef * (
        1.0 + 3.0 * 0.044715 * value * value
    )
    return (activated, slope)


def contract_last(left, right):
    return lax.dot_general(
        left, right, (((1,), (1,)), ((), ())), preferred_element_type=jnp.float32
    )


def contract_first(left, right):
    return lax.dot_general(
        left, right, (((0,), (0,)), ((), ())), preferred_element_type=jnp.float32
    )


def rows_kernel(core_ref, length_ref, inputs, gain, cot, normed, masked, mine, inverse):
    wide = inputs[...].astype(jnp.float32)
    inv = lax.rsqrt(jnp.mean(wide * wide, axis=-1, keepdims=True) + 1e-06)
    inverse[...] = inv
    normed[...] = (wide * inv * gain[...]).astype(jnp.bfloat16)
    valid = lax.broadcasted_iota(jnp.int32, (SEQ, 1), 0) < length_ref[0]
    masked[...] = (cot[...].astype(jnp.float32) * valid.astype(jnp.float32)).astype(jnp.bfloat16)
    for half in range(2):
        rows = pl.ds(pl.multiple_of(core_ref[0] * 96 + half * 48, 16), 48)
        mine[half, 0] = normed[rows, :]
        mine[half, 1] = masked[rows, :]


def own_rows(core, lengths, inputs, gain, cot):
    smem = pl.BlockSpec(memory_space=pltpu.SMEM)
    vmem = pl.BlockSpec(memory_space=pltpu.VMEM)
    return pl.pallas_call(
        rows_kernel,
        in_specs=[smem, smem, vmem, vmem, vmem],
        out_shape=[
            jax.ShapeDtypeStruct((SEQ, D), jnp.bfloat16),
            jax.ShapeDtypeStruct((SEQ, D), jnp.bfloat16),
            jax.ShapeDtypeStruct((2, 2, 48, D), jnp.bfloat16),
            jax.ShapeDtypeStruct((SEQ, 1), jnp.float32),
        ],
        compiler_params=pltpu.CompilerParams(vmem_limit_bytes=58 * 2**20),
    )(core, lengths, inputs, gain, cot)


def own_kernel(
    start_ref, own_ref, normed, masked, inputs, inverse, gain, gate_hbm, up_hbm, down_hbm, feats,
    units, hidden, dgate, dup, kept, sent, normed_cut, cot_cut, own_cot,
    gate_w, up_w, down_w, gate, up_proj, branch, dnormed, turned, sems,
):
    loads = [
        pltpu.make_async_copy(source, into, sems.at[at])
        for at, (source, into) in enumerate(
            ((gate_hbm, gate_w), (up_hbm, up_w), (down_hbm, down_w))
        )
    ]
    for load in loads:
        load.start()
    window = pl.ds(pl.multiple_of(start_ref[0], 128), WINDOW)
    normed_cut[...] = normed[:, window]
    cot_cut[...] = masked[:, window]
    turned[...] = masked[...].astype(jnp.float32).T
    own_cot[...] = turned[pl.ds(pl.multiple_of(own_ref[0] * OWN, 16), OWN), :]

    def split_dirs(dirs):
        high = dirs.astype(jnp.bfloat16).astype(jnp.float32)
        return jnp.concatenate([high, dirs - high]).astype(jnp.bfloat16)

    def onto(array, dirs):
        both = contract_last(array[...], split_dirs(dirs))
        return both[:, :K] + both[:, K:]

    tiles = [slice(at, at + TILE) for at in range(0, UNITS, TILE)]
    wide_tiles = [slice(at, at + 768) for at in range(0, D, 768)]
    loads[0].wait()
    for tile in tiles:
        gate[:, tile] = jnp.dot(normed[...], gate_w[:, tile], preferred_element_type=jnp.float32)
    loads[1].wait()
    for tile in tiles:
        up_proj[:, tile] = jnp.dot(normed[...], up_w[:, tile], preferred_element_type=jnp.float32)
    loads[2].wait()
    for tile in tiles:
        dhidden = contract_last(masked[...], down_w[tile, :])
        activated, slope = gelu_pair(gate[:, tile])
        up_tile = up_proj[:, tile]
        hidden[:, tile] = (activated * up_tile).astype(jnp.bfloat16)
        dgate[:, tile] = (dhidden * up_tile * slope).astype(jnp.bfloat16)
        dup[:, tile] = (dhidden * activated).astype(jnp.bfloat16)
    for tile in wide_tiles:
        branch[:, tile] = jnp.dot(hidden[...], down_w[:, tile], preferred_element_type=jnp.float32)
    for tile in wide_tiles:
        dnormed[:, tile] = contract_last(dgate[...], gate_w[tile, :]) + contract_last(
            dup[...], up_w[tile, :]
        )
    loss = jnp.sum(
        onto(dgate, units[0]) * onto(normed, feats[0])
        + onto(dup, units[1]) * onto(normed, feats[1])
        + onto(hidden, units[2]) * onto(masked, feats[2]),
        axis=0,
        keepdims=True,
    )
    wide = inputs[...].astype(jnp.float32)
    inv = inverse[...]
    gained = dnormed[...] * gain[...]
    back = gained * inv - wide * (inv * inv * inv) * jnp.mean(
        gained * wide, axis=-1, keepdims=True
    )
    branch_t = branch[...].T.astype(jnp.bfloat16)
    back_t = back.T.astype(jnp.bfloat16)
    loss_rows = jnp.broadcast_to(loss, (16, K)).astype(jnp.bfloat16)
    first_core = lax.rem(own_ref[0], 2) == 0
    for place in range(8):
        t = place % 2 * 8 + place // 2 * 2
        for into, low_first in ((kept, first_core), (sent, jnp.logical_not(first_core))):
            for at, array in enumerate((back_t, branch_t)):
                into[place, at * OWN : (at + 1) * OWN, :SEQ] = jnp.where(
                    low_first,
                    array[t * OWN : (t + 1) * OWN],
                    array[(t + 1) * OWN : (t + 2) * OWN],
                )
            into[place, :, SEQ:] = jnp.zeros((ROWS, LANES - SEQ), jnp.bfloat16)
            into[place, 2 * OWN :, :SEQ] = jnp.zeros((16, SEQ), jnp.bfloat16)
            into[place, 2 * OWN :, :K] = loss_rows


def own_work(start, own_at, normed, masked, inputs, inverse, gain, w_gate, w_up, w_down, feats, units):
    smem = pl.BlockSpec(memory_space=pltpu.SMEM)
    vmem = pl.BlockSpec(memory_space=pltpu.VMEM)
    far = pl.BlockSpec(memory_space=pl.ANY)
    return pl.pallas_call(
        own_kernel,
        in_specs=[smem] * 2 + [vmem] * 5 + [far] * 3 + [vmem] * 2,
        out_shape=[jax.ShapeDtypeStruct((SEQ, UNITS), jnp.bfloat16)] * 3
        + [jax.ShapeDtypeStruct((8, ROWS, LANES), jnp.bfloat16)] * 2
        + [jax.ShapeDtypeStruct((SEQ, WINDOW), jnp.bfloat16)] * 2
        + [jax.ShapeDtypeStruct((OWN, SEQ), jnp.float32)],
        scratch_shapes=[
            pltpu.VMEM((D, UNITS), jnp.bfloat16),
            pltpu.VMEM((D, UNITS), jnp.bfloat16),
            pltpu.VMEM((UNITS, D), jnp.bfloat16),
            pltpu.VMEM((SEQ, UNITS), jnp.float32),
            pltpu.VMEM((SEQ, UNITS), jnp.float32),
            pltpu.VMEM((SEQ, D), jnp.float32),
            pltpu.VMEM((SEQ, D), jnp.float32),
            pltpu.VMEM((D, SEQ), jnp.float32),
            pltpu.SemaphoreType.DMA((3,)),
        ],
        compiler_params=pltpu.CompilerParams(vmem_limit_bytes=58 * 2**20),
        cost_estimate=pl.CostEstimate(
            flops=10 * SEQ * D * UNITS, bytes_accessed=7 * D * UNITS, transcendentals=SEQ * UNITS
        ),
    )(start, own_at, normed, masked, inputs, inverse, gain, w_gate, w_up, w_down, feats, units)


def unit_kernel(pieces, count, start_ref, *refs):
    sources, refs = refs[:count], refs[count:]
    weights, outs, cuts, refs = refs[:3], refs[3:6], refs[6:8], refs[8:]
    normed, cot, gate_w, up_w, down_w, gate, up_proj, hidden, dgate, dup = refs[:10]
    sems, weight_sems, out_sems = refs[10:]
    row_copies = ([], [])
    row = 0
    for at, (src, item, size) in enumerate(pieces):
        for which, into in enumerate((normed, cot)):
            row_copies[which].append(
                pltpu.make_async_copy(
                    sources[src].at[item, which],
                    into.at[pl.ds(row, size)],
                    sems.at[2 * at + which],
                )
            )
        row += size
    loads = [
        pltpu.make_async_copy(weight, into, weight_sems.at[at])
        for at, (weight, into) in enumerate(zip(weights, (gate_w, up_w, down_w)))
    ]
    for copy in row_copies[0] + loads[:2] + row_copies[1] + loads[2:]:
        copy.start()
    window = pl.ds(pl.multiple_of(start_ref[0], 128), WINDOW)
    tiles = [slice(at, at + TILE) for at in range(0, UNITS, TILE)]
    for copy in row_copies[0] + loads[:1]:
        copy.wait()
    for tile in tiles:
        gate[:, tile] = jnp.dot(normed[...], gate_w[:, tile], preferred_element_type=jnp.float32)
    cuts[0][...] = normed[:, window]
    loads[1].wait()
    for tile in tiles:
        up_proj[:, tile] = jnp.dot(normed[...], up_w[:, tile], preferred_element_type=jnp.float32)
    for copy in row_copies[1] + loads[2:]:
        copy.wait()
    cuts[1][...] = cot[:, window]
    stores = []
    for tile in tiles:
        dhidden = contract_last(cot[...], down_w[tile, :])
        activated, slope = gelu_pair(gate[:, tile])
        up_tile = up_proj[:, tile]
        hidden[:, tile] = (activated * up_tile).astype(jnp.bfloat16)
        dgate[:, tile] = (dhidden * up_tile * slope).astype(jnp.bfloat16)
        dup[:, tile] = (dhidden * activated).astype(jnp.bfloat16)
        for source, into in zip((hidden, dgate, dup), outs):
            store = pltpu.make_async_copy(
                source.at[:, tile], into.at[:, tile], out_sems.at[len(stores)]
            )
            store.start()
            stores.append(store)
    for store in stores:
        store.wait()


def unit_work(start, sources, pieces, w_gate, w_up, w_down):
    rows = sum(piece[2] for piece in pieces)
    far = pl.BlockSpec(memory_space=pl.ANY)
    vmem = pl.BlockSpec(memory_space=pltpu.VMEM)
    by_unit = pltpu.VMEM((rows, UNITS), jnp.bfloat16)
    return pl.pallas_call(
        functools.partial(unit_kernel, pieces, len(sources)),
        in_specs=[pl.BlockSpec(memory_space=pltpu.SMEM)] + [far] * (len(sources) + 3),
        out_specs=[far] * 3 + [vmem] * 2,
        out_shape=[jax.ShapeDtypeStruct((rows, UNITS), jnp.bfloat16)] * 3
        + [jax.ShapeDtypeStruct((rows, WINDOW), jnp.bfloat16)] * 2,
        scratch_shapes=[
            pltpu.VMEM((rows, D), jnp.bfloat16),
            pltpu.VMEM((rows, D), jnp.bfloat16),
            pltpu.VMEM((D, UNITS), jnp.bfloat16),
            pltpu.VMEM((D, UNITS), jnp.bfloat16),
            pltpu.VMEM((UNITS, D), jnp.bfloat16),
            pltpu.VMEM((rows, UNITS), jnp.float32),
            pltpu.VMEM((rows, UNITS), jnp.float32),
            by_unit,
            by_unit,
            by_unit,
            pltpu.SemaphoreType.DMA((2 * len(pieces),)),
            pltpu.SemaphoreType.DMA((3,)),
            pltpu.SemaphoreType.DMA((3 * UNITS // TILE,)),
        ],
        compiler_params=pltpu.CompilerParams(vmem_limit_bytes=58 * 2**20),
        cost_estimate=pl.CostEstimate(
            flops=6 * rows * D * UNITS,
            bytes_accessed=6 * D * UNITS + 4 * rows * D + 6 * rows * UNITS,
            transcendentals=rows * UNITS,
        ),
    )(start, *sources, w_gate, w_up, w_down)


def grad_kernel(owners, sizes, offset_ref, scale_ref, *refs):
    groups, refs = refs[: 5 * len(sizes)], refs[5 * len(sizes) :]
    outs, (hidden, dgate, dup, left, right, wide, sems) = refs[:3], refs[3:]
    copies = {}
    for which, into in ((1, dgate), (2, dup), (0, hidden)):
        row = 0
        for at, size in enumerate(sizes):
            copy = pltpu.make_async_copy(
                groups[5 * at + which], into.at[pl.ds(row, size)], sems.at[3 * at + which]
            )
            copy.start()
            copies[which, at] = copy
            row += size
    row = 0
    for at in range(len(sizes)):
        inside = 0
        for owner, size in owners[at]:
            scale = scale_ref[owner]
            here, there = pl.ds(inside, size), pl.ds(row, size)
            for side, into in ((3, left), (4, right)):
                into[there, :] = (
                    groups[5 * at + side][here, :].astype(jnp.float32) * scale
                ).astype(jnp.bfloat16)
            inside += size
            row += size
    offset = pl.multiple_of(offset_ref[0], 32)
    place = 0
    for which, factor, array, out in (
        (1, left, dgate, outs[0]),
        (2, left, dup, outs[1]),
        (0, right, hidden, outs[2]),
    ):
        for at in range(len(sizes)):
            copies[which, at].wait()
        for start in range(0, UNITS, TILE):
            tile = slice(start, start + TILE)
            wide[place % 3] = contract_first(factor[...], array[:, tile])
            out[:, tile] = wide[place % 3, pl.ds(offset, SLICE), :].astype(jnp.bfloat16)
            place += 1


def grad_work(offset, scales, groups, owners):
    sizes = [group[0].shape[0] for group in groups]
    rows = sum(sizes)
    far = pl.BlockSpec(memory_space=pl.ANY)
    vmem = pl.BlockSpec(memory_space=pltpu.VMEM)
    return pl.pallas_call(
        functools.partial(grad_kernel, owners, sizes),
        in_specs=[pl.BlockSpec(memory_space=pltpu.SMEM)] * 2
        + ([far] * 3 + [vmem] * 2) * len(sizes),
        out_shape=[jax.ShapeDtypeStruct((SLICE, UNITS), jnp.bfloat16)] * 3,
        scratch_shapes=[
            pltpu.VMEM((rows, UNITS), jnp.bfloat16),
            pltpu.VMEM((rows, UNITS), jnp.bfloat16),
            pltpu.VMEM((rows, UNITS), jnp.bfloat16),
            pltpu.VMEM((rows, WINDOW), jnp.bfloat16),
            pltpu.VMEM((rows, WINDOW), jnp.bfloat16),
            pltpu.VMEM((3, WINDOW, TILE), jnp.float32),
            pltpu.SemaphoreType.DMA((3 * len(sizes),)),
        ],
        compiler_params=pltpu.CompilerParams(vmem_limit_bytes=58 * 2**20),
        cost_estimate=pl.CostEstimate(
            flops=6 * rows * WINDOW * UNITS,
            bytes_accessed=6 * rows * UNITS + 6 * SLICE * UNITS + 4 * rows * WINDOW,
            transcendentals=0,
        ),
    )(offset, scales, *[array for group in groups for array in group])


def pick(array, index):
    return lax.dynamic_index_in_dim(array, index, 0, keepdims=False)


def after(arrays, *earlier):
    return lax.optimization_barrier((arrays, earlier))[0]


def mix_kernel(y_ref, core_ref, inputs, *refs):
    pieces, mixed, total = refs[:8], refs[8], refs[9]
    for side in range(2):
        for step in range(4):
            piece = pieces[4 * side + step]
            y_at = lax.rem(y_ref[0] + step, 4)
            core = core_ref[0] if side == 0 else 1 - core_ref[0]
            for x_high in range(2):
                row = (x_high * 8 + y_at * 2 + core) * OWN
                total[pl.ds(pl.multiple_of(row, 16), OWN), :] = piece[x_high, :OWN, :SEQ].astype(
                    jnp.float32
                )
    mixed[...] = (inputs[...].astype(jnp.float32) + total[...].T).astype(jnp.bfloat16)


def mix(y_at, core, inputs, pieces):
    smem = pl.BlockSpec(memory_space=pltpu.SMEM)
    vmem = pl.BlockSpec(memory_space=pltpu.VMEM)
    return pl.pallas_call(
        mix_kernel,
        in_specs=[smem, smem] + [vmem] * 9,
        out_shape=jax.ShapeDtypeStruct((SEQ, D), jnp.bfloat16),
        scratch_shapes=[pltpu.VMEM((D, SEQ), jnp.float32)],
        compiler_params=pltpu.CompilerParams(vmem_limit_bytes=58 * 2**20),
    )(y_at, core, inputs, *pieces)


def shards(inputs, norm_gain, w_gate, w_up, w_down, feat_dirs, unit_dirs, cotangent, lengths):
    t_index = lax.axis_index("tensor")
    d_index = lax.axis_index("dp")
    core = t_index % 2
    y_at = (t_index // 2) % 4
    x_high = t_index // 8
    core_index = core.astype(jnp.int32)[None]
    rows = inputs.reshape(SEQ, D)
    gain = norm_gain[None, :]
    normed, masked, mine, inverse = own_rows(
        core_index, lengths, rows, gain, cotangent.reshape(SEQ, D)
    )

    from_pair = move(mine, to_pair)
    from_down = move(mine, to_up)
    from_up = move(mine, to_down)

    first_column = d_index * SLICE
    window_start = (first_column // 128 * 128).astype(jnp.int32)[None]
    window_offset = (first_column % 128).astype(jnp.int32)[None]
    *own, kept, sent, own_normed_cut, own_cot_cut, own_cot = own_work(
        window_start, t_index.astype(jnp.int32)[None], normed, masked, rows, inverse,
        gain, w_gate, w_up, w_down, feat_dirs, unit_dirs,
    )
    own = (*own, own_normed_cut, own_cot_cut)

    from_pair, from_down, from_up, kept, sent = after(
        (from_pair, from_down, from_up, kept, sent), own
    )
    kept_sibling = move(sent, to_sibling)
    x_second = move(from_down, to_pair)
    up_second = move(from_down, to_up)
    down_second = move(from_pair, to_down)
    first_sources = [(a, move(a, to_sibling)) for a in (from_pair, from_down, from_up)]
    kept = kept.astype(jnp.float32) + kept_sibling.astype(jnp.float32)
    kept = kept.astype(jnp.bfloat16).reshape(4, 2, ROWS, LANES)
    arrived = [move(pick(kept, (y_at + step) % 4), along_y(step)) for step in (1, 2, 3)]
    total = pick(kept, y_at)

    def group_of(sources, owners):
        pieces = []
        flat = []
        for at, (pair, owner) in enumerate(zip(sources, owners)):
            for which in range(2):
                for item in range(pair[0].shape[0]):
                    pieces.append((2 * at + which, item, 48))
                    flat.append((owner, 48))
        arrays = [a for pair in sources for a in pair]
        worked = unit_work(window_start, arrays, tuple(pieces), w_gate, w_up, w_down)
        return worked, tuple(flat)

    first_sources = after(first_sources, total)
    first, owners_first = group_of(first_sources, (1, 2, 4))

    arrived, total, x_second, up_second, down_second = after(
        (arrived, total, x_second, up_second, down_second), first
    )
    third = [move(x_second[:1], to_up), move(down_second[1:], to_down)]
    second_sources = [(a, move(a, to_sibling)) for a in (x_second, up_second, down_second)]
    total = sum((a.astype(jnp.float32) for a in arrived), total.astype(jnp.float32))
    total = total.astype(jnp.bfloat16)
    total_far = move(total, to_far)

    second, owners_second = group_of(second_sources, (3, 6, 5))

    total, total_far, third = after((total, total_far, third), second)
    third_sources = [(a, move(a, to_sibling)) for a in third]
    total = total.astype(jnp.float32) + total_far.astype(jnp.float32)
    loss_dot = total[:1, 2 * OWN, :K]
    bound = 0.5 * math.sqrt(SEQ * D * FF)
    own_ratio = jnp.sqrt(jnp.mean(loss_dot * loss_dot, axis=1)) / bound
    scale = 1.0 / (N_DP * jnp.maximum(own_ratio, 1.0))
    scale_row = jnp.broadcast_to(scale[None, :], (1, 128))
    scale_pair = move(scale_row, to_pair)
    branch = total[:, OWN:].astype(jnp.bfloat16)
    branches = [branch] + [move(branch, along_y(-step)) for step in (1, 2, 3)]

    third, owners_third = group_of(third_sources, (7, 7))

    scale_pair, branches = after((scale_pair, branches), third)
    two = jnp.concatenate([scale_row, scale_pair], axis=0)
    two_down = move(two, along_z(1))
    two_up = move(two, along_z(-1))
    two_far = move(two, along_z(2))
    siblings = [move(a, to_sibling) for a in branches]
    own_back = pick(total, x_high)[:OWN, :SEQ]
    grad_input = ((own_back + own_cot) * scale).astype(jnp.bfloat16).T.reshape(1, SEQ, OWN)

    scales = jnp.concatenate([two[:, 0], two_down[:, 0], two_up[:, 0], two_far[:, 0]])
    grads = grad_work(
        window_offset,
        scales,
        (own, first, second, third),
        (((0, SEQ),), owners_first, owners_second, owners_third),
    )
    branches, siblings = after((branches, siblings), grads)
    mixed = mix(
        y_at.astype(jnp.int32)[None], core_index, rows, branches + siblings
    ).reshape(1, SEQ, D)
    every_loss = jnp.stack([a[0, OWN, :K] for a in branches + siblings])
    shared_loss = pick(every_loss, (4 - y_at) % 4 + 4 * core).astype(jnp.float32)[None, :]
    norm_ratio = jnp.sqrt(jnp.mean(shared_loss * shared_loss, axis=1)) / bound
    return (mixed, norm_ratio, grad_input, grads[0], grads[1], grads[2].T)


def solution(mesh):
    placed = (
        P("dp", None, None),
        P(),
        P(None, "tensor"),
        P(None, "tensor"),
        P("tensor", None),
        P(),
        P(None, None, "tensor"),
        P("dp", None, None),
        P("dp"),
    )
    return jax.shard_map(
        shards,
        mesh=mesh,
        in_specs=placed,
        out_specs=(
            P("dp", None, None),
            P("dp"),
            P("dp", None, "tensor"),
            P("dp", "tensor"),
            P("dp", "tensor"),
            P("tensor", "dp"),
        ),
        check_vma=False,
    )
```

```python
import functools
import math

import jax
import jax.numpy as jnp
from jax import lax
from jax.experimental import pallas as pl
from jax.experimental.pallas import tpu as pltpu
from jax.sharding import PartitionSpec as P

D = 2304
FF = 18432
SEQ = 192
K = 8
N_DP = 8
N_T = 16
UNITS = FF // N_T
SLICE = D // N_DP
OWN = D // N_T
BOTH = ("dp", "tensor")
TILE = 256
WINDOW = 384
LANES = 256
ROWS = 2 * OWN + 16


def device_index(x, y, z, core):
    x, y, z = x % 4, y % 4, z % 4
    return ((x % 2) * 4 + z) * N_T + ((x // 2) * 4 + y) * 2 + core


def move(array, target):
    pairs = [
        (device_index(x, y, z, core), device_index(*target(x, y, z, core)))
        for x in range(4)
        for y in range(4)
        for z in range(4)
        for core in range(2)
    ]
    return lax.ppermute(array, BOTH, pairs)


def to_pair(x, y, z, core):
    return (x ^ 1, y, z, core)


def to_up(x, y, z, core):
    return (x, y, z + 1, core)


def to_down(x, y, z, core):
    return (x, y, z - 1, core)


def to_sibling(x, y, z, core):
    return (x, y, z, 1 - core)


def to_far(x, y, z, core):
    return (x ^ 2, y, z, core)


def along_y(step):
    return lambda x, y, z, core: (x, y + step, z, core)


def along_z(step):
    return lambda x, y, z, core: (x, y, z + step, core)


def gelu_pair(value):
    coef = math.sqrt(2.0 / math.pi)
    tangent = jnp.tanh(coef * (value + 0.044715 * value * value * value))
    activated = 0.5 * value * (1.0 + tangent)
    slope = 0.5 * (1.0 + tangent) + 0.5 * value * (1.0 - tangent * tangent) * coef * (
        1.0 + 3.0 * 0.044715 * value * value
    )
    return (activated, slope)


def contract_last(left, right):
    return lax.dot_general(
        left, right, (((1,), (1,)), ((), ())), preferred_element_type=jnp.float32
    )


def contract_first(left, right):
    return lax.dot_general(
        left, right, (((0,), (0,)), ((), ())), preferred_element_type=jnp.float32
    )


def rows_kernel(core_ref, length_ref, inputs, gain, cot, normed, masked, mine, inverse):
    wide = inputs[...].astype(jnp.float32)
    inv = lax.rsqrt(jnp.mean(wide * wide, axis=-1, keepdims=True) + 1e-06)
    inverse[...] = inv
    normed[...] = (wide * inv * gain[...]).astype(jnp.bfloat16)
    valid = lax.broadcasted_iota(jnp.int32, (SEQ, 1), 0) < length_ref[0]
    masked[...] = (cot[...].astype(jnp.float32) * valid.astype(jnp.float32)).astype(jnp.bfloat16)
    for half in range(2):
        rows = pl.ds(pl.multiple_of(core_ref[0] * 96 + half * 48, 16), 48)
        mine[half, 0] = normed[rows, :]
        mine[half, 1] = masked[rows, :]


def own_rows(core, lengths, inputs, gain, cot):
    smem = pl.BlockSpec(memory_space=pltpu.SMEM)
    vmem = pl.BlockSpec(memory_space=pltpu.VMEM)
    return pl.pallas_call(
        rows_kernel,
        in_specs=[smem, smem, vmem, vmem, vmem],
        out_shape=[
            jax.ShapeDtypeStruct((SEQ, D), jnp.bfloat16),
            jax.ShapeDtypeStruct((SEQ, D), jnp.bfloat16),
            jax.ShapeDtypeStruct((2, 2, 48, D), jnp.bfloat16),
            jax.ShapeDtypeStruct((SEQ, 1), jnp.float32),
        ],
        compiler_params=pltpu.CompilerParams(vmem_limit_bytes=58 * 2**20),
    )(core, lengths, inputs, gain, cot)


def own_kernel(
    start_ref, own_ref, normed, masked, inputs, inverse, gain, gate_hbm, up_hbm, down_hbm, feats,
    units, hidden, dgate, dup, kept, sent, normed_cut, cot_cut, own_cot,
    gate_w, up_w, down_w, gate, up_proj, branch, dnormed, turned, sems,
):
    loads = [
        pltpu.make_async_copy(source, into, sems.at[at])
        for at, (source, into) in enumerate(
            ((gate_hbm, gate_w), (up_hbm, up_w), (down_hbm, down_w))
        )
    ]
    for load in loads:
        load.start()
    window = pl.ds(pl.multiple_of(start_ref[0], 128), WINDOW)
    normed_cut[...] = normed[:, window]
    cot_cut[...] = masked[:, window]
    turned[...] = masked[...].astype(jnp.float32).T
    own_cot[...] = turned[pl.ds(pl.multiple_of(own_ref[0] * OWN, 16), OWN), :]

    def split_dirs(dirs):
        high = dirs.astype(jnp.bfloat16).astype(jnp.float32)
        return jnp.concatenate([high, dirs - high]).astype(jnp.bfloat16)

    def onto(array, dirs):
        both = contract_last(array[...], split_dirs(dirs))
        return both[:, :K] + both[:, K:]

    tiles = [slice(at, min(at + TILE, UNITS)) for at in range(0, UNITS, TILE)]
    wide_tiles = [slice(at, at + 768) for at in range(0, D, 768)]
    loads[0].wait()
    for tile in tiles:
        gate[:, tile] = jnp.dot(normed[...], gate_w[:, tile], preferred_element_type=jnp.float32)
    loads[1].wait()
    for tile in tiles:
        up_proj[:, tile] = jnp.dot(normed[...], up_w[:, tile], preferred_element_type=jnp.float32)
    loads[2].wait()
    for tile in tiles:
        dhidden = contract_last(masked[...], down_w[tile, :])
        activated, slope = gelu_pair(gate[:, tile])
        up_tile = up_proj[:, tile]
        hidden[:, tile] = (activated * up_tile).astype(jnp.bfloat16)
        dgate[:, tile] = (dhidden * up_tile * slope).astype(jnp.bfloat16)
        dup[:, tile] = (dhidden * activated).astype(jnp.bfloat16)
    for tile in wide_tiles:
        branch[:, tile] = jnp.dot(hidden[...], down_w[:, tile], preferred_element_type=jnp.float32)
    for tile in wide_tiles:
        dnormed[:, tile] = contract_last(dgate[...], gate_w[tile, :]) + contract_last(
            dup[...], up_w[tile, :]
        )
    loss = jnp.sum(
        onto(dgate, units[0]) * onto(normed, feats[0])
        + onto(dup, units[1]) * onto(normed, feats[1])
        + onto(hidden, units[2]) * onto(masked, feats[2]),
        axis=0,
        keepdims=True,
    )
    wide = inputs[...].astype(jnp.float32)
    inv = inverse[...]
    gained = dnormed[...] * gain[...]
    back = gained * inv - wide * (inv * inv * inv) * jnp.mean(
        gained * wide, axis=-1, keepdims=True
    )
    branch_t = branch[...].T.astype(jnp.bfloat16)
    back_t = back.T.astype(jnp.bfloat16)
    loss_rows = jnp.broadcast_to(loss, (16, K)).astype(jnp.bfloat16)
    first_core = lax.rem(own_ref[0], 2) == 0
    for place in range(8):
        t = place % 2 * 8 + place // 2 * 2
        for into, low_first in ((kept, first_core), (sent, jnp.logical_not(first_core))):
            for at, array in enumerate((back_t, branch_t)):
                into[place, at * OWN : (at + 1) * OWN, :SEQ] = jnp.where(
                    low_first,
                    array[t * OWN : (t + 1) * OWN],
                    array[(t + 1) * OWN : (t + 2) * OWN],
                )
            into[place, :, SEQ:] = jnp.zeros((ROWS, LANES - SEQ), jnp.bfloat16)
            into[place, 2 * OWN :, :SEQ] = jnp.zeros((16, SEQ), jnp.bfloat16)
            into[place, 2 * OWN :, :K] = loss_rows


def own_work(start, own_at, normed, masked, inputs, inverse, gain, w_gate, w_up, w_down, feats, units):
    smem = pl.BlockSpec(memory_space=pltpu.SMEM)
    vmem = pl.BlockSpec(memory_space=pltpu.VMEM)
    far = pl.BlockSpec(memory_space=pl.ANY)
    return pl.pallas_call(
        own_kernel,
        in_specs=[smem] * 2 + [vmem] * 5 + [far] * 3 + [vmem] * 2,
        out_shape=[jax.ShapeDtypeStruct((SEQ, UNITS), jnp.bfloat16)] * 3
        + [jax.ShapeDtypeStruct((8, ROWS, LANES), jnp.bfloat16)] * 2
        + [jax.ShapeDtypeStruct((SEQ, WINDOW), jnp.bfloat16)] * 2
        + [jax.ShapeDtypeStruct((OWN, SEQ), jnp.float32)],
        scratch_shapes=[
            pltpu.VMEM((D, UNITS), jnp.bfloat16),
            pltpu.VMEM((D, UNITS), jnp.bfloat16),
            pltpu.VMEM((UNITS, D), jnp.bfloat16),
            pltpu.VMEM((SEQ, UNITS), jnp.float32),
            pltpu.VMEM((SEQ, UNITS), jnp.float32),
            pltpu.VMEM((SEQ, D), jnp.float32),
            pltpu.VMEM((SEQ, D), jnp.float32),
            pltpu.VMEM((D, SEQ), jnp.float32),
            pltpu.SemaphoreType.DMA((3,)),
        ],
        compiler_params=pltpu.CompilerParams(vmem_limit_bytes=58 * 2**20),
        cost_estimate=pl.CostEstimate(
            flops=10 * SEQ * D * UNITS, bytes_accessed=7 * D * UNITS, transcendentals=SEQ * UNITS
        ),
    )(start, own_at, normed, masked, inputs, inverse, gain, w_gate, w_up, w_down, feats, units)


def unit_kernel(pieces, count, start_ref, *refs):
    sources, refs = refs[:count], refs[count:]
    weights, outs, cuts, refs = refs[:3], refs[3:6], refs[6:8], refs[8:]
    normed, cot, gate_w, up_w, down_w, gate, up_proj, hidden, dgate, dup = refs[:10]
    sems, weight_sems, out_sems = refs[10:]
    row_copies = ([], [])
    row = 0
    for at, (src, item, size) in enumerate(pieces):
        for which, into in enumerate((normed, cot)):
            row_copies[which].append(
                pltpu.make_async_copy(
                    sources[src].at[item, which],
                    into.at[pl.ds(row, size)],
                    sems.at[2 * at + which],
                )
            )
        row += size
    loads = [
        pltpu.make_async_copy(weight, into, weight_sems.at[at])
        for at, (weight, into) in enumerate(zip(weights, (gate_w, up_w, down_w)))
    ]
    for copy in row_copies[0] + loads[:2] + row_copies[1] + loads[2:]:
        copy.start()
    window = pl.ds(pl.multiple_of(start_ref[0], 128), WINDOW)
    tiles = [slice(at, min(at + TILE, UNITS)) for at in range(0, UNITS, TILE)]
    for copy in row_copies[0] + loads[:1]:
        copy.wait()
    for tile in tiles:
        gate[:, tile] = jnp.dot(normed[...], gate_w[:, tile], preferred_element_type=jnp.float32)
    cuts[0][...] = normed[:, window]
    loads[1].wait()
    for tile in tiles:
        up_proj[:, tile] = jnp.dot(normed[...], up_w[:, tile], preferred_element_type=jnp.float32)
    for copy in row_copies[1] + loads[2:]:
        copy.wait()
    cuts[1][...] = cot[:, window]
    stores = []
    for tile in tiles:
        dhidden = contract_last(cot[...], down_w[tile, :])
        activated, slope = gelu_pair(gate[:, tile])
        up_tile = up_proj[:, tile]
        hidden[:, tile] = (activated * up_tile).astype(jnp.bfloat16)
        dgate[:, tile] = (dhidden * up_tile * slope).astype(jnp.bfloat16)
        dup[:, tile] = (dhidden * activated).astype(jnp.bfloat16)
        for source, into in zip((hidden, dgate, dup), outs):
            store = pltpu.make_async_copy(
                source.at[:, tile], into.at[:, tile], out_sems.at[len(stores)]
            )
            store.start()
            stores.append(store)
    for store in stores:
        store.wait()


def unit_work(start, sources, pieces, w_gate, w_up, w_down):
    rows = sum(piece[2] for piece in pieces)
    far = pl.BlockSpec(memory_space=pl.ANY)
    vmem = pl.BlockSpec(memory_space=pltpu.VMEM)
    by_unit = pltpu.VMEM((rows, UNITS), jnp.bfloat16)
    return pl.pallas_call(
        functools.partial(unit_kernel, pieces, len(sources)),
        in_specs=[pl.BlockSpec(memory_space=pltpu.SMEM)] + [far] * (len(sources) + 3),
        out_specs=[far] * 3 + [vmem] * 2,
        out_shape=[jax.ShapeDtypeStruct((rows, UNITS), jnp.bfloat16)] * 3
        + [jax.ShapeDtypeStruct((rows, WINDOW), jnp.bfloat16)] * 2,
        scratch_shapes=[
            pltpu.VMEM((rows, D), jnp.bfloat16),
            pltpu.VMEM((rows, D), jnp.bfloat16),
            pltpu.VMEM((D, UNITS), jnp.bfloat16),
            pltpu.VMEM((D, UNITS), jnp.bfloat16),
            pltpu.VMEM((UNITS, D), jnp.bfloat16),
            pltpu.VMEM((rows, UNITS), jnp.float32),
            pltpu.VMEM((rows, UNITS), jnp.float32),
            by_unit,
            by_unit,
            by_unit,
            pltpu.SemaphoreType.DMA((2 * len(pieces),)),
            pltpu.SemaphoreType.DMA((3,)),
            pltpu.SemaphoreType.DMA((3 * -(-UNITS // TILE),)),
        ],
        compiler_params=pltpu.CompilerParams(vmem_limit_bytes=58 * 2**20),
        cost_estimate=pl.CostEstimate(
            flops=6 * rows * D * UNITS,
            bytes_accessed=6 * D * UNITS + 4 * rows * D + 6 * rows * UNITS,
            transcendentals=rows * UNITS,
        ),
    )(start, *sources, w_gate, w_up, w_down)


def grad_kernel(owners, sizes, offset_ref, scale_ref, *refs):
    groups, refs = refs[: 5 * len(sizes)], refs[5 * len(sizes) :]
    outs, (hidden, dgate, dup, left, right, wide, sems) = refs[:3], refs[3:]
    copies = {}
    for which, into in ((1, dgate), (2, dup), (0, hidden)):
        row = 0
        for at, size in enumerate(sizes):
            copy = pltpu.make_async_copy(
                groups[5 * at + which], into.at[pl.ds(row, size)], sems.at[3 * at + which]
            )
            copy.start()
            copies[which, at] = copy
            row += size
    row = 0
    for at in range(len(sizes)):
        inside = 0
        for owner, size in owners[at]:
            scale = scale_ref[owner]
            here, there = pl.ds(inside, size), pl.ds(row, size)
            for side, into in ((3, left), (4, right)):
                into[there, :] = (
                    groups[5 * at + side][here, :].astype(jnp.float32) * scale
                ).astype(jnp.bfloat16)
            inside += size
            row += size
    offset = pl.multiple_of(offset_ref[0], 32)
    place = 0
    for which, factor, array, out in (
        (1, left, dgate, outs[0]),
        (2, left, dup, outs[1]),
        (0, right, hidden, outs[2]),
    ):
        for at in range(len(sizes)):
            copies[which, at].wait()
        for start in range(0, UNITS, TILE):
            tile = slice(start, min(start + TILE, UNITS))
            columns = slice(0, tile.stop - tile.start)
            wide[place % 3, :, columns] = contract_first(factor[...], array[:, tile])
            out[:, tile] = wide[place % 3, pl.ds(offset, SLICE), columns].astype(jnp.bfloat16)
            place += 1


def grad_work(offset, scales, groups, owners):
    sizes = [group[0].shape[0] for group in groups]
    rows = sum(sizes)
    far = pl.BlockSpec(memory_space=pl.ANY)
    vmem = pl.BlockSpec(memory_space=pltpu.VMEM)
    return pl.pallas_call(
        functools.partial(grad_kernel, owners, sizes),
        in_specs=[pl.BlockSpec(memory_space=pltpu.SMEM)] * 2
        + ([far] * 3 + [vmem] * 2) * len(sizes),
        out_shape=[jax.ShapeDtypeStruct((SLICE, UNITS), jnp.bfloat16)] * 3,
        scratch_shapes=[
            pltpu.VMEM((rows, UNITS), jnp.bfloat16),
            pltpu.VMEM((rows, UNITS), jnp.bfloat16),
            pltpu.VMEM((rows, UNITS), jnp.bfloat16),
            pltpu.VMEM((rows, WINDOW), jnp.bfloat16),
            pltpu.VMEM((rows, WINDOW), jnp.bfloat16),
            pltpu.VMEM((3, WINDOW, TILE), jnp.float32),
            pltpu.SemaphoreType.DMA((3 * len(sizes),)),
        ],
        compiler_params=pltpu.CompilerParams(vmem_limit_bytes=58 * 2**20),
        cost_estimate=pl.CostEstimate(
            flops=6 * rows * WINDOW * UNITS,
            bytes_accessed=6 * rows * UNITS + 6 * SLICE * UNITS + 4 * rows * WINDOW,
            transcendentals=0,
        ),
    )(offset, scales, *[array for group in groups for array in group])


def pick(array, index):
    return lax.dynamic_index_in_dim(array, index, 0, keepdims=False)


def after(arrays, *earlier):
    return lax.optimization_barrier((arrays, earlier))[0]


def mix_kernel(y_ref, core_ref, inputs, *refs):
    pieces, mixed, total = refs[:8], refs[8], refs[9]
    for side in range(2):
        for step in range(4):
            piece = pieces[4 * side + step]
            y_at = lax.rem(y_ref[0] + step, 4)
            core = core_ref[0] if side == 0 else 1 - core_ref[0]
            for x_high in range(2):
                row = (x_high * 8 + y_at * 2 + core) * OWN
                total[pl.ds(pl.multiple_of(row, 16), OWN), :] = piece[x_high, :OWN, :SEQ].astype(
                    jnp.float32
                )
    mixed[...] = (inputs[...].astype(jnp.float32) + total[...].T).astype(jnp.bfloat16)


def mix(y_at, core, inputs, pieces):
    smem = pl.BlockSpec(memory_space=pltpu.SMEM)
    vmem = pl.BlockSpec(memory_space=pltpu.VMEM)
    return pl.pallas_call(
        mix_kernel,
        in_specs=[smem, smem] + [vmem] * 9,
        out_shape=jax.ShapeDtypeStruct((SEQ, D), jnp.bfloat16),
        scratch_shapes=[pltpu.VMEM((D, SEQ), jnp.float32)],
        compiler_params=pltpu.CompilerParams(vmem_limit_bytes=24 * 2**20),
    )(y_at, core, inputs, *pieces)


def shards(inputs, norm_gain, w_gate, w_up, w_down, feat_dirs, unit_dirs, cotangent, lengths):
    t_index = lax.axis_index("tensor")
    d_index = lax.axis_index("dp")
    core = t_index % 2
    y_at = (t_index // 2) % 4
    x_high = t_index // 8
    core_index = core.astype(jnp.int32)[None]
    rows = inputs.reshape(SEQ, D)
    gain = norm_gain[None, :]
    normed, masked, mine, inverse = own_rows(
        core_index, lengths, rows, gain, cotangent.reshape(SEQ, D)
    )

    from_pair = move(mine, to_pair)
    from_down = move(mine, to_up)
    from_up = move(mine, to_down)

    first_column = d_index * SLICE
    window_start = (first_column // 128 * 128).astype(jnp.int32)[None]
    window_offset = (first_column % 128).astype(jnp.int32)[None]
    *own, kept, sent, own_normed_cut, own_cot_cut, own_cot = own_work(
        window_start, t_index.astype(jnp.int32)[None], normed, masked, rows, inverse,
        gain, w_gate, w_up, w_down, feat_dirs, unit_dirs,
    )
    own = (*own, own_normed_cut, own_cot_cut)

    from_pair, from_down, from_up, kept, sent = after(
        (from_pair, from_down, from_up, kept, sent), own
    )
    kept_sibling = move(sent, to_sibling)
    x_second = move(from_down, to_pair)
    up_second = move(from_down, to_up)
    down_second = move(from_pair, to_down)
    first_sources = [(a, move(a, to_sibling)) for a in (from_pair, from_down, from_up)]
    kept = kept.astype(jnp.float32) + kept_sibling.astype(jnp.float32)
    kept = kept.astype(jnp.bfloat16).reshape(4, 2, ROWS, LANES)
    arrived = [move(pick(kept, (y_at + step) % 4), along_y(step)) for step in (2, 1)]
    last_piece = pick(kept, (y_at + 3) % 4)
    total = pick(kept, y_at)

    def group_of(sources, owners):
        pieces = []
        flat = []
        for at, (pair, owner) in enumerate(zip(sources, owners)):
            for which in range(2):
                for item in range(pair[0].shape[0]):
                    pieces.append((2 * at + which, item, 48))
                    flat.append((owner, 48))
        arrays = [a for pair in sources for a in pair]
        worked = unit_work(window_start, arrays, tuple(pieces), w_gate, w_up, w_down)
        return worked, tuple(flat)

    first_sources = after(first_sources, total)
    first, owners_first = group_of(first_sources, (1, 2, 4))

    arrived, total, last_piece, x_second, up_second, down_second = after(
        (arrived, total, last_piece, x_second, up_second, down_second), first
    )
    arrived.append(move(last_piece, along_y(3)))
    third = [move(x_second[:1], to_up), move(down_second[1:], to_down)]
    second_sources = [(a, move(a, to_sibling)) for a in (x_second, up_second, down_second)]
    total = sum((a.astype(jnp.float32) for a in arrived), total.astype(jnp.float32))
    total = total.astype(jnp.bfloat16)
    total_far = move(total, to_far)

    second, owners_second = group_of(second_sources, (3, 6, 5))

    total, total_far, third = after((total, total_far, third), second)
    third_sources = [(a, move(a, to_sibling)) for a in third]
    total = total.astype(jnp.float32) + total_far.astype(jnp.float32)
    loss_dot = total[:1, 2 * OWN, :K]
    bound = 0.5 * math.sqrt(SEQ * D * FF)
    own_ratio = jnp.sqrt(jnp.mean(loss_dot * loss_dot, axis=1)) / bound
    scale = 1.0 / (N_DP * jnp.maximum(own_ratio, 1.0))
    scale_row = jnp.broadcast_to(scale[None, :], (1, 128))
    scale_pair = move(scale_row, to_pair)
    branch = total[:, OWN:].astype(jnp.bfloat16)
    branches = [branch] + [move(branch, along_y(-step)) for step in (1, 2, 3)]

    third, owners_third = group_of(third_sources, (7, 7))

    scale_pair, branches = after((scale_pair, branches), third)
    two = jnp.concatenate([scale_row, scale_pair], axis=0)
    two_down = move(two, along_z(1))
    two_up = move(two, along_z(-1))
    two_far = move(two, along_z(2))
    siblings = [move(a, to_sibling) for a in branches]
    own_back = pick(total, x_high)[:OWN, :SEQ]
    grad_input = ((own_back + own_cot) * scale).astype(jnp.bfloat16).T.reshape(1, SEQ, OWN)

    scales = jnp.concatenate([two[:, 0], two_down[:, 0], two_up[:, 0], two_far[:, 0]])
    grads = grad_work(
        window_offset,
        scales,
        (own, first, second, third),
        (((0, SEQ),), owners_first, owners_second, owners_third),
    )
    branches, siblings = after((branches, siblings), grads)
    mixed = mix(
        y_at.astype(jnp.int32)[None], core_index, rows, branches + siblings
    ).reshape(1, SEQ, D)
    every_loss = jnp.stack([a[0, OWN, :K] for a in branches + siblings])
    shared_loss = pick(every_loss, (4 - y_at) % 4 + 4 * core).astype(jnp.float32)[None, :]
    norm_ratio = jnp.sqrt(jnp.mean(shared_loss * shared_loss, axis=1)) / bound
    return (mixed, norm_ratio, grad_input, grads[0], grads[1], grads[2].T)


def solution(mesh):
    placed = (
        P("dp", None, None),
        P(),
        P(None, "tensor"),
        P(None, "tensor"),
        P("tensor", None),
        P(),
        P(None, None, "tensor"),
        P("dp", None, None),
        P("dp"),
    )
    return jax.shard_map(
        shards,
        mesh=mesh,
        in_specs=placed,
        out_specs=(
            P("dp", None, None),
            P("dp"),
            P("dp", None, "tensor"),
            P("dp", "tensor"),
            P("dp", "tensor"),
            P("tensor", "dp"),
        ),
        check_vma=False,
    )
```

```python
import functools
import math

import jax
import jax.numpy as jnp
from jax import lax
from jax.experimental import pallas as pl
from jax.experimental.pallas import tpu as pltpu
from jax.sharding import PartitionSpec as P

D = 2304
FF = 18432
SEQ = 192
K = 8
N_DP = 8
N_T = 16
UNITS = FF // N_T
SLICE = D // N_DP
OWN = D // N_T
BOTH = ("dp", "tensor")
TILE = 256
WINDOW = 384
LANES = 256
ROWS = 2 * OWN + 16


def device_index(x, y, z, core):
    x, y, z = x % 4, y % 4, z % 4
    return ((x % 2) * 4 + z) * N_T + ((x // 2) * 4 + y) * 2 + core


def move(array, target):
    pairs = [
        (device_index(x, y, z, core), device_index(*target(x, y, z, core)))
        for x in range(4)
        for y in range(4)
        for z in range(4)
        for core in range(2)
    ]
    return lax.ppermute(array, BOTH, pairs)


def to_pair(x, y, z, core):
    return (x ^ 1, y, z, core)


def to_up(x, y, z, core):
    return (x, y, z + 1, core)


def to_down(x, y, z, core):
    return (x, y, z - 1, core)


def to_sibling(x, y, z, core):
    return (x, y, z, 1 - core)


def to_far(x, y, z, core):
    return (x ^ 2, y, z, core)


def along_y(step):
    return lambda x, y, z, core: (x, y + step, z, core)


def along_z(step):
    return lambda x, y, z, core: (x, y, z + step, core)


def gelu_pair(value):
    coef = math.sqrt(2.0 / math.pi)
    tangent = jnp.tanh(coef * (value + 0.044715 * value * value * value))
    activated = 0.5 * value * (1.0 + tangent)
    slope = 0.5 * (1.0 + tangent) + 0.5 * value * (1.0 - tangent * tangent) * coef * (
        1.0 + 3.0 * 0.044715 * value * value
    )
    return (activated, slope)


def contract_last(left, right):
    return lax.dot_general(
        left, right, (((1,), (1,)), ((), ())), preferred_element_type=jnp.float32
    )


def contract_first(left, right):
    return lax.dot_general(
        left, right, (((0,), (0,)), ((), ())), preferred_element_type=jnp.float32
    )


def rows_kernel(core_ref, length_ref, inputs, gain, cot, normed, masked, mine, inverse):
    wide = inputs[...].astype(jnp.float32)
    inv = lax.rsqrt(jnp.mean(wide * wide, axis=-1, keepdims=True) + 1e-06)
    inverse[...] = inv
    normed[...] = (wide * inv * gain[...]).astype(jnp.bfloat16)
    valid = lax.broadcasted_iota(jnp.int32, (SEQ, 1), 0) < length_ref[0]
    masked[...] = (cot[...].astype(jnp.float32) * valid.astype(jnp.float32)).astype(jnp.bfloat16)
    for half in range(2):
        rows = pl.ds(pl.multiple_of(core_ref[0] * 96 + half * 48, 16), 48)
        mine[half, 0] = normed[rows, :]
        mine[half, 1] = masked[rows, :]


def own_rows(core, lengths, inputs, gain, cot):
    smem = pl.BlockSpec(memory_space=pltpu.SMEM)
    vmem = pl.BlockSpec(memory_space=pltpu.VMEM)
    return pl.pallas_call(
        rows_kernel,
        in_specs=[smem, smem, vmem, vmem, vmem],
        out_shape=[
            jax.ShapeDtypeStruct((SEQ, D), jnp.bfloat16),
            jax.ShapeDtypeStruct((SEQ, D), jnp.bfloat16),
            jax.ShapeDtypeStruct((2, 2, 48, D), jnp.bfloat16),
            jax.ShapeDtypeStruct((SEQ, 1), jnp.float32),
        ],
        compiler_params=pltpu.CompilerParams(vmem_limit_bytes=58 * 2**20),
    )(core, lengths, inputs, gain, cot)


def own_kernel(
    start_ref, own_ref, normed, masked, inputs, inverse, gain, gate_hbm, up_hbm, down_hbm, feats,
    units, hidden, dgate, dup, kept, sent, normed_cut, cot_cut, own_cot,
    gate_w, up_w, down_w, gate, up_proj, branch, dnormed, turned, sems,
):
    loads = [
        pltpu.make_async_copy(source, into, sems.at[at])
        for at, (source, into) in enumerate(
            ((gate_hbm, gate_w), (up_hbm, up_w), (down_hbm, down_w))
        )
    ]
    loads[0].start()
    window = pl.ds(pl.multiple_of(start_ref[0], 128), WINDOW)
    normed_cut[...] = normed[:, window]
    cot_cut[...] = masked[:, window]
    turned[...] = masked[...].astype(jnp.float32).T
    own_cot[...] = turned[pl.ds(pl.multiple_of(own_ref[0] * OWN, 16), OWN), :]

    def split_dirs(dirs):
        high = dirs.astype(jnp.bfloat16).astype(jnp.float32)
        return jnp.concatenate([high, dirs - high]).astype(jnp.bfloat16)

    def onto(array, dirs):
        both = contract_last(array[...], split_dirs(dirs))
        return both[:, :K] + both[:, K:]

    tiles = [slice(at, min(at + TILE, UNITS)) for at in range(0, UNITS, TILE)]
    wide_tiles = [slice(at, at + 768) for at in range(0, D, 768)]
    loads[0].wait()
    loads[1].start()
    loads[2].start()
    for tile in tiles:
        gate[:, tile] = jnp.dot(normed[...], gate_w[:, tile], preferred_element_type=jnp.float32)
    loads[1].wait()
    for tile in tiles:
        up_proj[:, tile] = jnp.dot(normed[...], up_w[:, tile], preferred_element_type=jnp.float32)
    loads[2].wait()
    for tile in tiles:
        dhidden = contract_last(masked[...], down_w[tile, :])
        activated, slope = gelu_pair(gate[:, tile])
        up_tile = up_proj[:, tile]
        hidden[:, tile] = (activated * up_tile).astype(jnp.bfloat16)
        dgate[:, tile] = (dhidden * up_tile * slope).astype(jnp.bfloat16)
        dup[:, tile] = (dhidden * activated).astype(jnp.bfloat16)
    for tile in wide_tiles:
        branch[:, tile] = jnp.dot(hidden[...], down_w[:, tile], preferred_element_type=jnp.float32)
    for tile in wide_tiles:
        dnormed[:, tile] = contract_last(dgate[...], gate_w[tile, :]) + contract_last(
            dup[...], up_w[tile, :]
        )
    loss = jnp.sum(
        onto(dgate, units[0]) * onto(normed, feats[0])
        + onto(dup, units[1]) * onto(normed, feats[1])
        + onto(hidden, units[2]) * onto(masked, feats[2]),
        axis=0,
        keepdims=True,
    )
    wide = inputs[...].astype(jnp.float32)
    inv = inverse[...]
    gained = dnormed[...] * gain[...]
    back = gained * inv - wide * (inv * inv * inv) * jnp.mean(
        gained * wide, axis=-1, keepdims=True
    )
    branch_t = branch[...].T.astype(jnp.bfloat16)
    back_t = back.T.astype(jnp.bfloat16)
    loss_rows = jnp.broadcast_to(loss, (16, K)).astype(jnp.bfloat16)
    first_core = lax.rem(own_ref[0], 2) == 0
    for place in range(8):
        t = place % 2 * 8 + place // 2 * 2
        for into, low_first in ((kept, first_core), (sent, jnp.logical_not(first_core))):
            for at, array in enumerate((back_t, branch_t)):
                into[place, at * OWN : (at + 1) * OWN, :SEQ] = jnp.where(
                    low_first,
                    array[t * OWN : (t + 1) * OWN],
                    array[(t + 1) * OWN : (t + 2) * OWN],
                )
            into[place, :, SEQ:] = jnp.zeros((ROWS, LANES - SEQ), jnp.bfloat16)
            into[place, 2 * OWN :, :SEQ] = jnp.zeros((16, SEQ), jnp.bfloat16)
            into[place, 2 * OWN :, :K] = loss_rows


def own_work(start, own_at, normed, masked, inputs, inverse, gain, w_gate, w_up, w_down, feats, units):
    smem = pl.BlockSpec(memory_space=pltpu.SMEM)
    vmem = pl.BlockSpec(memory_space=pltpu.VMEM)
    far = pl.BlockSpec(memory_space=pl.ANY)
    return pl.pallas_call(
        own_kernel,
        in_specs=[smem] * 2 + [vmem] * 5 + [far] * 3 + [vmem] * 2,
        out_shape=[jax.ShapeDtypeStruct((SEQ, UNITS), jnp.bfloat16)] * 3
        + [jax.ShapeDtypeStruct((8, ROWS, LANES), jnp.bfloat16)] * 2
        + [jax.ShapeDtypeStruct((SEQ, WINDOW), jnp.bfloat16)] * 2
        + [jax.ShapeDtypeStruct((OWN, SEQ), jnp.float32)],
        scratch_shapes=[
            pltpu.VMEM((D, UNITS), jnp.bfloat16),
            pltpu.VMEM((D, UNITS), jnp.bfloat16),
            pltpu.VMEM((UNITS, D), jnp.bfloat16),
            pltpu.VMEM((SEQ, UNITS), jnp.float32),
            pltpu.VMEM((SEQ, UNITS), jnp.float32),
            pltpu.VMEM((SEQ, D), jnp.float32),
            pltpu.VMEM((SEQ, D), jnp.float32),
            pltpu.VMEM((D, SEQ), jnp.float32),
            pltpu.SemaphoreType.DMA((3,)),
        ],
        compiler_params=pltpu.CompilerParams(vmem_limit_bytes=58 * 2**20),
        cost_estimate=pl.CostEstimate(
            flops=10 * SEQ * D * UNITS, bytes_accessed=7 * D * UNITS, transcendentals=SEQ * UNITS
        ),
    )(start, own_at, normed, masked, inputs, inverse, gain, w_gate, w_up, w_down, feats, units)


def unit_kernel(pieces, count, start_ref, *refs):
    sources, refs = refs[:count], refs[count:]
    weights, outs, cuts, refs = refs[:3], refs[3:6], refs[6:8], refs[8:]
    normed, cot, gate_w, up_w, down_w, gate, up_proj, hidden, dgate, dup = refs[:10]
    sems, weight_sems, out_sems = refs[10:]
    row_copies = ([], [])
    row = 0
    for at, (src, item, size) in enumerate(pieces):
        for which, into in enumerate((normed, cot)):
            row_copies[which].append(
                pltpu.make_async_copy(
                    sources[src].at[item, which],
                    into.at[pl.ds(row, size)],
                    sems.at[2 * at + which],
                )
            )
        row += size
    loads = [
        pltpu.make_async_copy(weight, into, weight_sems.at[at])
        for at, (weight, into) in enumerate(zip(weights, (gate_w, up_w, down_w)))
    ]
    for copy in row_copies[0] + loads[:1]:
        copy.start()
    window = pl.ds(pl.multiple_of(start_ref[0], 128), WINDOW)
    tiles = [slice(at, min(at + TILE, UNITS)) for at in range(0, UNITS, TILE)]
    for copy in row_copies[0] + loads[:1]:
        copy.wait()
    for copy in loads[1:2] + row_copies[1] + loads[2:]:
        copy.start()
    for tile in tiles:
        gate[:, tile] = jnp.dot(normed[...], gate_w[:, tile], preferred_element_type=jnp.float32)
    cuts[0][...] = normed[:, window]
    loads[1].wait()
    for tile in tiles:
        up_proj[:, tile] = jnp.dot(normed[...], up_w[:, tile], preferred_element_type=jnp.float32)
    for copy in row_copies[1] + loads[2:]:
        copy.wait()
    cuts[1][...] = cot[:, window]
    stores = []
    for tile in tiles:
        dhidden = contract_last(cot[...], down_w[tile, :])
        activated, slope = gelu_pair(gate[:, tile])
        up_tile = up_proj[:, tile]
        hidden[:, tile] = (activated * up_tile).astype(jnp.bfloat16)
        dgate[:, tile] = (dhidden * up_tile * slope).astype(jnp.bfloat16)
        dup[:, tile] = (dhidden * activated).astype(jnp.bfloat16)
        for source, into in zip((hidden, dgate, dup), outs):
            store = pltpu.make_async_copy(
                source.at[:, tile], into.at[:, tile], out_sems.at[len(stores)]
            )
            store.start()
            stores.append(store)
    for store in stores:
        store.wait()


def unit_work(start, sources, pieces, w_gate, w_up, w_down):
    rows = sum(piece[2] for piece in pieces)
    far = pl.BlockSpec(memory_space=pl.ANY)
    vmem = pl.BlockSpec(memory_space=pltpu.VMEM)
    by_unit = pltpu.VMEM((rows, UNITS), jnp.bfloat16)
    return pl.pallas_call(
        functools.partial(unit_kernel, pieces, len(sources)),
        in_specs=[pl.BlockSpec(memory_space=pltpu.SMEM)] + [far] * (len(sources) + 3),
        out_specs=[far] * 3 + [vmem] * 2,
        out_shape=[jax.ShapeDtypeStruct((rows, UNITS), jnp.bfloat16)] * 3
        + [jax.ShapeDtypeStruct((rows, WINDOW), jnp.bfloat16)] * 2,
        scratch_shapes=[
            pltpu.VMEM((rows, D), jnp.bfloat16),
            pltpu.VMEM((rows, D), jnp.bfloat16),
            pltpu.VMEM((D, UNITS), jnp.bfloat16),
            pltpu.VMEM((D, UNITS), jnp.bfloat16),
            pltpu.VMEM((UNITS, D), jnp.bfloat16),
            pltpu.VMEM((rows, UNITS), jnp.float32),
            pltpu.VMEM((rows, UNITS), jnp.float32),
            by_unit,
            by_unit,
            by_unit,
            pltpu.SemaphoreType.DMA((2 * len(pieces),)),
            pltpu.SemaphoreType.DMA((3,)),
            pltpu.SemaphoreType.DMA((3 * -(-UNITS // TILE),)),
        ],
        compiler_params=pltpu.CompilerParams(vmem_limit_bytes=58 * 2**20),
        cost_estimate=pl.CostEstimate(
            flops=6 * rows * D * UNITS,
            bytes_accessed=6 * D * UNITS + 4 * rows * D + 6 * rows * UNITS,
            transcendentals=rows * UNITS,
        ),
    )(start, *sources, w_gate, w_up, w_down)


def grad_kernel(owners, sizes, offset_ref, scale_ref, *refs):
    groups, refs = refs[: 5 * len(sizes)], refs[5 * len(sizes) :]
    outs, (hidden, dgate, dup, left, right, wide, sems) = refs[:3], refs[3:]
    copies = {}
    for which, into in ((1, dgate), (2, dup), (0, hidden)):
        row = 0
        for at, size in enumerate(sizes):
            copy = pltpu.make_async_copy(
                groups[5 * at + which], into.at[pl.ds(row, size)], sems.at[3 * at + which]
            )
            copies[which, at] = copy
            row += size
            if which == 1:
                copy.start()
    row = 0
    for at in range(len(sizes)):
        inside = 0
        for owner, size in owners[at]:
            scale = scale_ref[owner]
            here, there = pl.ds(inside, size), pl.ds(row, size)
            for side, into in ((3, left), (4, right)):
                into[there, :] = (
                    groups[5 * at + side][here, :].astype(jnp.float32) * scale
                ).astype(jnp.bfloat16)
            inside += size
            row += size
    offset = pl.multiple_of(offset_ref[0], 32)
    place = 0
    for which, factor, array, out in (
        (1, left, dgate, outs[0]),
        (2, left, dup, outs[1]),
        (0, right, hidden, outs[2]),
    ):
        for at in range(len(sizes)):
            copies[which, at].wait()
        if which == 1:
            for later in (2, 0):
                for at in range(len(sizes)):
                    copies[later, at].start()
        for start in range(0, UNITS, TILE):
            tile = slice(start, min(start + TILE, UNITS))
            columns = slice(0, tile.stop - tile.start)
            wide[place % 3, :, columns] = contract_first(factor[...], array[:, tile])
            out[:, tile] = wide[place % 3, pl.ds(offset, SLICE), columns].astype(jnp.bfloat16)
            place += 1


def grad_work(offset, scales, groups, owners):
    sizes = [group[0].shape[0] for group in groups]
    rows = sum(sizes)
    far = pl.BlockSpec(memory_space=pl.ANY)
    vmem = pl.BlockSpec(memory_space=pltpu.VMEM)
    return pl.pallas_call(
        functools.partial(grad_kernel, owners, sizes),
        in_specs=[pl.BlockSpec(memory_space=pltpu.SMEM)] * 2
        + ([far] * 3 + [vmem] * 2) * len(sizes),
        out_shape=[jax.ShapeDtypeStruct((SLICE, UNITS), jnp.bfloat16)] * 3,
        scratch_shapes=[
            pltpu.VMEM((rows, UNITS), jnp.bfloat16),
            pltpu.VMEM((rows, UNITS), jnp.bfloat16),
            pltpu.VMEM((rows, UNITS), jnp.bfloat16),
            pltpu.VMEM((rows, WINDOW), jnp.bfloat16),
            pltpu.VMEM((rows, WINDOW), jnp.bfloat16),
            pltpu.VMEM((3, WINDOW, TILE), jnp.float32),
            pltpu.SemaphoreType.DMA((3 * len(sizes),)),
        ],
        compiler_params=pltpu.CompilerParams(vmem_limit_bytes=58 * 2**20),
        cost_estimate=pl.CostEstimate(
            flops=6 * rows * WINDOW * UNITS,
            bytes_accessed=6 * rows * UNITS + 6 * SLICE * UNITS + 4 * rows * WINDOW,
            transcendentals=0,
        ),
    )(offset, scales, *[array for group in groups for array in group])


def pick(array, index):
    return lax.dynamic_index_in_dim(array, index, 0, keepdims=False)


def after(arrays, *earlier):
    return lax.optimization_barrier((arrays, earlier))[0]


def mix_kernel(y_ref, core_ref, inputs, *refs):
    pieces, mixed, total = refs[:8], refs[8], refs[9]
    for side in range(2):
        for step in range(4):
            piece = pieces[4 * side + step]
            y_at = lax.rem(y_ref[0] + step, 4)
            core = core_ref[0] if side == 0 else 1 - core_ref[0]
            for x_high in range(2):
                row = (x_high * 8 + y_at * 2 + core) * OWN
                total[pl.ds(pl.multiple_of(row, 16), OWN), :] = piece[x_high, :OWN, :SEQ].astype(
                    jnp.float32
                )
    mixed[...] = (inputs[...].astype(jnp.float32) + total[...].T).astype(jnp.bfloat16)


def mix(y_at, core, inputs, pieces):
    smem = pl.BlockSpec(memory_space=pltpu.SMEM)
    vmem = pl.BlockSpec(memory_space=pltpu.VMEM)
    return pl.pallas_call(
        mix_kernel,
        in_specs=[smem, smem] + [vmem] * 9,
        out_shape=jax.ShapeDtypeStruct((SEQ, D), jnp.bfloat16),
        scratch_shapes=[pltpu.VMEM((D, SEQ), jnp.float32)],
        compiler_params=pltpu.CompilerParams(vmem_limit_bytes=24 * 2**20),
    )(y_at, core, inputs, *pieces)


def shards(inputs, norm_gain, w_gate, w_up, w_down, feat_dirs, unit_dirs, cotangent, lengths):
    t_index = lax.axis_index("tensor")
    d_index = lax.axis_index("dp")
    core = t_index % 2
    y_at = (t_index // 2) % 4
    x_high = t_index // 8
    core_index = core.astype(jnp.int32)[None]
    rows = inputs.reshape(SEQ, D)
    gain = norm_gain[None, :]
    normed, masked, mine, inverse = own_rows(
        core_index, lengths, rows, gain, cotangent.reshape(SEQ, D)
    )

    from_pair = move(mine, to_pair)
    from_down = move(mine, to_up)
    from_up = move(mine, to_down)

    first_column = d_index * SLICE
    window_start = (first_column // 128 * 128).astype(jnp.int32)[None]
    window_offset = (first_column % 128).astype(jnp.int32)[None]
    *own, kept, sent, own_normed_cut, own_cot_cut, own_cot = own_work(
        window_start, t_index.astype(jnp.int32)[None], normed, masked, rows, inverse,
        gain, w_gate, w_up, w_down, feat_dirs, unit_dirs,
    )
    own = (*own, own_normed_cut, own_cot_cut)

    from_pair, from_down, from_up, kept, sent = after(
        (from_pair, from_down, from_up, kept, sent), own
    )
    kept_sibling = move(sent, to_sibling)
    x_second = move(from_down, to_pair)
    up_second = move(from_down, to_up)
    down_second = move(from_pair, to_down)
    first_sources = [(a, move(a, to_sibling)) for a in (from_pair, from_down, from_up)]
    kept = kept.astype(jnp.float32) + kept_sibling.astype(jnp.float32)
    kept = kept.astype(jnp.bfloat16).reshape(4, 2, ROWS, LANES)
    arrived = [move(pick(kept, (y_at + step) % 4), along_y(step)) for step in (2, 1)]
    last_piece = pick(kept, (y_at + 3) % 4)
    total = pick(kept, y_at)

    def group_of(sources, owners):
        pieces = []
        flat = []
        for at, (pair, owner) in enumerate(zip(sources, owners)):
            for which in range(2):
                for item in range(pair[0].shape[0]):
                    pieces.append((2 * at + which, item, 48))
                    flat.append((owner, 48))
        arrays = [a for pair in sources for a in pair]
        worked = unit_work(window_start, arrays, tuple(pieces), w_gate, w_up, w_down)
        return worked, tuple(flat)

    first_sources = after(first_sources, total)
    first, owners_first = group_of(first_sources, (1, 2, 4))

    arrived, total, last_piece, x_second, up_second, down_second = after(
        (arrived, total, last_piece, x_second, up_second, down_second), first
    )
    arrived.append(move(last_piece, along_y(3)))
    third = [move(x_second[:1], to_up), move(down_second[1:], to_down)]
    second_sources = [(a, move(a, to_sibling)) for a in (x_second, up_second, down_second)]
    total = sum((a.astype(jnp.float32) for a in arrived), total.astype(jnp.float32))
    total = total.astype(jnp.bfloat16)
    total_far = move(total, to_far)

    second, owners_second = group_of(second_sources, (3, 6, 5))

    total, total_far, third = after((total, total_far, third), second)
    third_sources = [(a, move(a, to_sibling)) for a in third]
    total = total.astype(jnp.float32) + total_far.astype(jnp.float32)
    loss_dot = total[:1, 2 * OWN, :K]
    bound = 0.5 * math.sqrt(SEQ * D * FF)
    own_ratio = jnp.sqrt(jnp.mean(loss_dot * loss_dot, axis=1)) / bound
    scale = 1.0 / (N_DP * jnp.maximum(own_ratio, 1.0))
    scale_row = jnp.broadcast_to(scale[None, :], (1, 128))
    scale_pair = move(scale_row, to_pair)
    branch = total[:, OWN:].astype(jnp.bfloat16)
    branches = [branch] + [move(branch, along_y(-step)) for step in (1, 2, 3)]

    third, owners_third = group_of(third_sources, (7, 7))

    scale_pair, branches = after((scale_pair, branches), third)
    two = jnp.concatenate([scale_row, scale_pair], axis=0)
    two_down = move(two, along_z(1))
    two_up = move(two, along_z(-1))
    two_far = move(two, along_z(2))
    siblings = [move(a, to_sibling) for a in branches]
    own_back = pick(total, x_high)[:OWN, :SEQ]
    grad_input = ((own_back + own_cot) * scale).astype(jnp.bfloat16).T.reshape(1, SEQ, OWN)

    scales = jnp.concatenate([two[:, 0], two_down[:, 0], two_up[:, 0], two_far[:, 0]])
    grads = grad_work(
        window_offset,
        scales,
        (own, first, second, third),
        (((0, SEQ),), owners_first, owners_second, owners_third),
    )
    branches, siblings = after((branches, siblings), grads)
    mixed = mix(
        y_at.astype(jnp.int32)[None], core_index, rows, branches + siblings
    ).reshape(1, SEQ, D)
    every_loss = jnp.stack([a[0, OWN, :K] for a in branches + siblings])
    shared_loss = pick(every_loss, (4 - y_at) % 4 + 4 * core).astype(jnp.float32)[None, :]
    norm_ratio = jnp.sqrt(jnp.mean(shared_loss * shared_loss, axis=1)) / bound
    return (mixed, norm_ratio, grad_input, grads[0], grads[1], grads[2].T)


def solution(mesh):
    placed = (
        P("dp", None, None),
        P(),
        P(None, "tensor"),
        P(None, "tensor"),
        P("tensor", None),
        P(),
        P(None, None, "tensor"),
        P("dp", None, None),
        P("dp"),
    )
    return jax.shard_map(
        shards,
        mesh=mesh,
        in_specs=placed,
        out_specs=(
            P("dp", None, None),
            P("dp"),
            P("dp", None, "tensor"),
            P("dp", "tensor"),
            P("dp", "tensor"),
            P("tensor", "dp"),
        ),
        check_vma=False,
    )
```

```python
import functools
import math

import jax
import jax.numpy as jnp
from jax import lax
from jax.experimental import pallas as pl
from jax.experimental.pallas import tpu as pltpu
from jax.sharding import PartitionSpec as P

D = 2304
FF = 18432
SEQ = 192
K = 8
N_DP = 8
N_T = 16
UNITS = FF // N_T
SLICE = D // N_DP
OWN = D // N_T
BOTH = ("dp", "tensor")
TILE = 256
WINDOW = 384
LANES = 256
ROWS = 2 * OWN + 16


def device_index(x, y, z, core):
    x, y, z = x % 4, y % 4, z % 4
    return ((x % 2) * 4 + z) * N_T + ((x // 2) * 4 + y) * 2 + core


def move(array, target):
    pairs = [
        (device_index(x, y, z, core), device_index(*target(x, y, z, core)))
        for x in range(4)
        for y in range(4)
        for z in range(4)
        for core in range(2)
    ]
    return lax.ppermute(array, BOTH, pairs)


def to_pair(x, y, z, core):
    return (x ^ 1, y, z, core)


def to_up(x, y, z, core):
    return (x, y, z + 1, core)


def to_down(x, y, z, core):
    return (x, y, z - 1, core)


def to_sibling(x, y, z, core):
    return (x, y, z, 1 - core)


def to_far(x, y, z, core):
    return (x ^ 2, y, z, core)


def along_y(step):
    return lambda x, y, z, core: (x, y + step, z, core)


def along_z(step):
    return lambda x, y, z, core: (x, y, z + step, core)


def gelu_pair(value):
    coef = math.sqrt(2.0 / math.pi)
    tangent = jnp.tanh(coef * (value + 0.044715 * value * value * value))
    activated = 0.5 * value * (1.0 + tangent)
    slope = 0.5 * (1.0 + tangent) + 0.5 * value * (1.0 - tangent * tangent) * coef * (
        1.0 + 3.0 * 0.044715 * value * value
    )
    return (activated, slope)


def contract_last(left, right):
    return lax.dot_general(
        left, right, (((1,), (1,)), ((), ())), preferred_element_type=jnp.float32
    )


def contract_first(left, right):
    return lax.dot_general(
        left, right, (((0,), (0,)), ((), ())), preferred_element_type=jnp.float32
    )


def as_row(ref):
    return jnp.concatenate([ref[at : at + 1, :] for at in range(D // 128)], axis=1)


def rows_kernel(core_ref, length_ref, inputs, gain, cot, normed, masked, mine, inverse):
    wide = inputs[...].astype(jnp.float32)
    inv = lax.rsqrt(jnp.mean(wide * wide, axis=-1, keepdims=True) + 1e-06)
    inverse[...] = inv
    normed[...] = (wide * inv * as_row(gain)).astype(jnp.bfloat16)
    valid = lax.broadcasted_iota(jnp.int32, (SEQ, 1), 0) < length_ref[0]
    masked[...] = (cot[...].astype(jnp.float32) * valid.astype(jnp.float32)).astype(jnp.bfloat16)
    for half in range(2):
        rows = pl.ds(pl.multiple_of(core_ref[0] * 96 + half * 48, 16), 48)
        mine[half, 0] = normed[rows, :]
        mine[half, 1] = masked[rows, :]


def own_rows(core, lengths, inputs, gain, cot):
    smem = pl.BlockSpec(memory_space=pltpu.SMEM)
    vmem = pl.BlockSpec(memory_space=pltpu.VMEM)
    return pl.pallas_call(
        rows_kernel,
        in_specs=[smem, smem, vmem, vmem, vmem],
        out_shape=[
            jax.ShapeDtypeStruct((SEQ, D), jnp.bfloat16),
            jax.ShapeDtypeStruct((SEQ, D), jnp.bfloat16),
            jax.ShapeDtypeStruct((2, 2, 48, D), jnp.bfloat16),
            jax.ShapeDtypeStruct((SEQ, 1), jnp.float32),
        ],
        compiler_params=pltpu.CompilerParams(vmem_limit_bytes=58 * 2**20),
    )(core, lengths, inputs, gain, cot)


def own_kernel(
    start_ref, own_ref, normed, masked, inputs, inverse, gain, gate_hbm, up_hbm, down_hbm, feats,
    units, hidden, dgate, dup, kept, sent, normed_cut, cot_cut, own_cot,
    gate_w, up_w, down_w, gate, up_proj, branch, dnormed, turned, sems,
):
    loads = [
        pltpu.make_async_copy(source, into, sems.at[at])
        for at, (source, into) in enumerate(
            ((gate_hbm, gate_w), (up_hbm, up_w), (down_hbm, down_w))
        )
    ]
    for load in loads:
        load.start()
    window = pl.ds(pl.multiple_of(start_ref[0], 128), WINDOW)
    normed_cut[...] = normed[:, window]
    cot_cut[...] = masked[:, window]
    turned[...] = masked[...].astype(jnp.float32).T
    own_cot[...] = turned[pl.ds(pl.multiple_of(own_ref[0] * OWN, 16), OWN), :]

    def split_dirs(dirs):
        high = dirs.astype(jnp.bfloat16).astype(jnp.float32)
        return jnp.concatenate([high, dirs - high]).astype(jnp.bfloat16)

    def onto(array, dirs):
        both = contract_last(array[...], split_dirs(dirs))
        return both[:, :K] + both[:, K:]

    tiles = [slice(at, min(at + TILE, UNITS)) for at in range(0, UNITS, TILE)]
    wide_tiles = [slice(at, at + 768) for at in range(0, D, 768)]
    loads[0].wait()
    for tile in tiles:
        gate[:, tile] = jnp.dot(normed[...], gate_w[:, tile], preferred_element_type=jnp.float32)
    loads[1].wait()
    for tile in tiles:
        up_proj[:, tile] = jnp.dot(normed[...], up_w[:, tile], preferred_element_type=jnp.float32)
    loads[2].wait()
    for tile in tiles:
        dhidden = contract_last(masked[...], down_w[tile, :])
        activated, slope = gelu_pair(gate[:, tile])
        up_tile = up_proj[:, tile]
        hidden[:, tile] = (activated * up_tile).astype(jnp.bfloat16)
        dgate[:, tile] = (dhidden * up_tile * slope).astype(jnp.bfloat16)
        dup[:, tile] = (dhidden * activated).astype(jnp.bfloat16)
    for tile in wide_tiles:
        branch[:, tile] = jnp.dot(hidden[...], down_w[:, tile], preferred_element_type=jnp.float32)
    for tile in wide_tiles:
        dnormed[:, tile] = contract_last(dgate[...], gate_w[tile, :]) + contract_last(
            dup[...], up_w[tile, :]
        )
    loss = jnp.sum(
        onto(dgate, units[0]) * onto(normed, feats[0])
        + onto(dup, units[1]) * onto(normed, feats[1])
        + onto(hidden, units[2]) * onto(masked, feats[2]),
        axis=0,
        keepdims=True,
    )
    wide = inputs[...].astype(jnp.float32)
    inv = inverse[...]
    gained = dnormed[...] * as_row(gain)
    back = gained * inv - wide * (inv * inv * inv) * jnp.mean(
        gained * wide, axis=-1, keepdims=True
    )
    branch_t = branch[...].T.astype(jnp.bfloat16)
    back_t = back.T.astype(jnp.bfloat16)
    loss_rows = jnp.broadcast_to(loss, (16, K)).astype(jnp.bfloat16)
    first_core = lax.rem(own_ref[0], 2) == 0
    for place in range(8):
        t = place % 2 * 8 + place // 2 * 2
        for into, low_first in ((kept, first_core), (sent, jnp.logical_not(first_core))):
            for at, array in enumerate((back_t, branch_t)):
                into[place, at * OWN : (at + 1) * OWN, :SEQ] = jnp.where(
                    low_first,
                    array[t * OWN : (t + 1) * OWN],
                    array[(t + 1) * OWN : (t + 2) * OWN],
                )
            into[place, :, SEQ:] = jnp.zeros((ROWS, LANES - SEQ), jnp.bfloat16)
            into[place, 2 * OWN :, :SEQ] = jnp.zeros((16, SEQ), jnp.bfloat16)
            into[place, 2 * OWN :, :K] = loss_rows


def own_work(start, own_at, normed, masked, inputs, inverse, gain, w_gate, w_up, w_down, feats, units):
    smem = pl.BlockSpec(memory_space=pltpu.SMEM)
    vmem = pl.BlockSpec(memory_space=pltpu.VMEM)
    far = pl.BlockSpec(memory_space=pl.ANY)
    return pl.pallas_call(
        own_kernel,
        in_specs=[smem] * 2 + [vmem] * 5 + [far] * 3 + [vmem] * 2,
        out_shape=[jax.ShapeDtypeStruct((SEQ, UNITS), jnp.bfloat16)] * 3
        + [jax.ShapeDtypeStruct((8, ROWS, LANES), jnp.bfloat16)] * 2
        + [jax.ShapeDtypeStruct((SEQ, WINDOW), jnp.bfloat16)] * 2
        + [jax.ShapeDtypeStruct((OWN, SEQ), jnp.float32)],
        scratch_shapes=[
            pltpu.VMEM((D, UNITS), jnp.bfloat16),
            pltpu.VMEM((D, UNITS), jnp.bfloat16),
            pltpu.VMEM((UNITS, D), jnp.bfloat16),
            pltpu.VMEM((SEQ, UNITS), jnp.float32),
            pltpu.VMEM((SEQ, UNITS), jnp.float32),
            pltpu.VMEM((SEQ, D), jnp.float32),
            pltpu.VMEM((SEQ, D), jnp.float32),
            pltpu.VMEM((D, SEQ), jnp.float32),
            pltpu.SemaphoreType.DMA((3,)),
        ],
        compiler_params=pltpu.CompilerParams(vmem_limit_bytes=58 * 2**20),
        cost_estimate=pl.CostEstimate(
            flops=10 * SEQ * D * UNITS, bytes_accessed=7 * D * UNITS, transcendentals=SEQ * UNITS
        ),
    )(start, own_at, normed, masked, inputs, inverse, gain, w_gate, w_up, w_down, feats, units)


def unit_kernel(pieces, count, start_ref, *refs):
    sources, refs = refs[:count], refs[count:]
    weights, outs, cuts, refs = refs[:3], refs[3:6], refs[6:8], refs[8:]
    normed, cot, gate_w, up_w, down_w, gate, up_proj, hidden, dgate, dup = refs[:10]
    sems, weight_sems, out_sems = refs[10:]
    row_copies = ([], [])
    row = 0
    for at, (src, item, size) in enumerate(pieces):
        for which, into in enumerate((normed, cot)):
            row_copies[which].append(
                pltpu.make_async_copy(
                    sources[src].at[item, which],
                    into.at[pl.ds(row, size)],
                    sems.at[2 * at + which],
                )
            )
        row += size
    loads = [
        pltpu.make_async_copy(weight, into, weight_sems.at[at])
        for at, (weight, into) in enumerate(zip(weights, (gate_w, up_w, down_w)))
    ]
    later = loads[1:2] + row_copies[1] + loads[2:]
    for copy in row_copies[0] + loads[:1] + (later if row <= SEQ else []):
        copy.start()
    window = pl.ds(pl.multiple_of(start_ref[0], 128), WINDOW)
    tiles = [slice(at, min(at + TILE, UNITS)) for at in range(0, UNITS, TILE)]
    for copy in row_copies[0] + loads[:1]:
        copy.wait()
    if row > SEQ:
        for copy in later:
            copy.start()
    for tile in tiles:
        gate[:, tile] = jnp.dot(normed[...], gate_w[:, tile], preferred_element_type=jnp.float32)
    cuts[0][...] = normed[:, window]
    loads[1].wait()
    for tile in tiles:
        up_proj[:, tile] = jnp.dot(normed[...], up_w[:, tile], preferred_element_type=jnp.float32)
    for copy in row_copies[1] + loads[2:]:
        copy.wait()
    cuts[1][...] = cot[:, window]
    stores = []
    for tile in tiles:
        dhidden = contract_last(cot[...], down_w[tile, :])
        activated, slope = gelu_pair(gate[:, tile])
        up_tile = up_proj[:, tile]
        hidden[:, tile] = (activated * up_tile).astype(jnp.bfloat16)
        dgate[:, tile] = (dhidden * up_tile * slope).astype(jnp.bfloat16)
        dup[:, tile] = (dhidden * activated).astype(jnp.bfloat16)
        for source, into in zip((hidden, dgate, dup), outs):
            store = pltpu.make_async_copy(
                source.at[:, tile], into.at[:, tile], out_sems.at[len(stores)]
            )
            store.start()
            stores.append(store)
    for store in stores:
        store.wait()


def unit_work(start, sources, pieces, w_gate, w_up, w_down):
    rows = sum(piece[2] for piece in pieces)
    far = pl.BlockSpec(memory_space=pl.ANY)
    vmem = pl.BlockSpec(memory_space=pltpu.VMEM)
    by_unit = pltpu.VMEM((rows, UNITS), jnp.bfloat16)
    return pl.pallas_call(
        functools.partial(unit_kernel, pieces, len(sources)),
        in_specs=[pl.BlockSpec(memory_space=pltpu.SMEM)] + [far] * (len(sources) + 3),
        out_specs=[far] * 3 + [vmem] * 2,
        out_shape=[jax.ShapeDtypeStruct((rows, UNITS), jnp.bfloat16)] * 3
        + [jax.ShapeDtypeStruct((rows, WINDOW), jnp.bfloat16)] * 2,
        scratch_shapes=[
            pltpu.VMEM((rows, D), jnp.bfloat16),
            pltpu.VMEM((rows, D), jnp.bfloat16),
            pltpu.VMEM((D, UNITS), jnp.bfloat16),
            pltpu.VMEM((D, UNITS), jnp.bfloat16),
            pltpu.VMEM((UNITS, D), jnp.bfloat16),
            pltpu.VMEM((rows, UNITS), jnp.float32),
            pltpu.VMEM((rows, UNITS), jnp.float32),
            by_unit,
            by_unit,
            by_unit,
            pltpu.SemaphoreType.DMA((2 * len(pieces),)),
            pltpu.SemaphoreType.DMA((3,)),
            pltpu.SemaphoreType.DMA((3 * -(-UNITS // TILE),)),
        ],
        compiler_params=pltpu.CompilerParams(vmem_limit_bytes=58 * 2**20),
        cost_estimate=pl.CostEstimate(
            flops=6 * rows * D * UNITS,
            bytes_accessed=6 * D * UNITS + 4 * rows * D + 6 * rows * UNITS,
            transcendentals=rows * UNITS,
        ),
    )(start, *sources, w_gate, w_up, w_down)


def grad_kernel(owners, sizes, offset_ref, scale_ref, *refs):
    groups, refs = refs[: 5 * len(sizes)], refs[5 * len(sizes) :]
    outs, (hidden, dgate, dup, left, right, wide, sems) = refs[:3], refs[3:]
    copies = {}
    for which, into in ((1, dgate), (2, dup), (0, hidden)):
        row = 0
        for at, size in enumerate(sizes):
            copy = pltpu.make_async_copy(
                groups[5 * at + which], into.at[pl.ds(row, size)], sems.at[3 * at + which]
            )
            copies[which, at] = copy
            row += size
            if which == 1:
                copy.start()
    row = 0
    for at in range(len(sizes)):
        inside = 0
        for owner, size in owners[at]:
            scale = scale_ref[owner]
            here, there = pl.ds(inside, size), pl.ds(row, size)
            for side, into in ((3, left), (4, right)):
                into[there, :] = (
                    groups[5 * at + side][here, :].astype(jnp.float32) * scale
                ).astype(jnp.bfloat16)
            inside += size
            row += size
    offset = pl.multiple_of(offset_ref[0], 32)
    place = 0
    for which, factor, array, out in (
        (1, left, dgate, outs[0]),
        (2, left, dup, outs[1]),
        (0, right, hidden, outs[2]),
    ):
        for at in range(len(sizes)):
            copies[which, at].wait()
        if which == 1:
            for later in (2, 0):
                for at in range(len(sizes)):
                    copies[later, at].start()
        for start in range(0, UNITS, TILE):
            tile = slice(start, min(start + TILE, UNITS))
            columns = slice(0, tile.stop - tile.start)
            wide[place % 3, :, columns] = contract_first(factor[...], array[:, tile])
            out[:, tile] = wide[place % 3, pl.ds(offset, SLICE), columns].astype(jnp.bfloat16)
            place += 1


def grad_work(offset, scales, groups, owners):
    sizes = [group[0].shape[0] for group in groups]
    rows = sum(sizes)
    far = pl.BlockSpec(memory_space=pl.ANY)
    vmem = pl.BlockSpec(memory_space=pltpu.VMEM)
    return pl.pallas_call(
        functools.partial(grad_kernel, owners, sizes),
        in_specs=[pl.BlockSpec(memory_space=pltpu.SMEM)] * 2
        + ([far] * 3 + [vmem] * 2) * len(sizes),
        out_shape=[jax.ShapeDtypeStruct((SLICE, UNITS), jnp.bfloat16)] * 3,
        scratch_shapes=[
            pltpu.VMEM((rows, UNITS), jnp.bfloat16),
            pltpu.VMEM((rows, UNITS), jnp.bfloat16),
            pltpu.VMEM((rows, UNITS), jnp.bfloat16),
            pltpu.VMEM((rows, WINDOW), jnp.bfloat16),
            pltpu.VMEM((rows, WINDOW), jnp.bfloat16),
            pltpu.VMEM((3, WINDOW, TILE), jnp.float32),
            pltpu.SemaphoreType.DMA((3 * len(sizes),)),
        ],
        compiler_params=pltpu.CompilerParams(vmem_limit_bytes=58 * 2**20),
        cost_estimate=pl.CostEstimate(
            flops=6 * rows * WINDOW * UNITS,
            bytes_accessed=6 * rows * UNITS + 6 * SLICE * UNITS + 4 * rows * WINDOW,
            transcendentals=0,
        ),
    )(offset, scales, *[array for group in groups for array in group])


def pick(array, index):
    return lax.dynamic_index_in_dim(array, index, 0, keepdims=False)


def after(arrays, *earlier):
    return lax.optimization_barrier((arrays, earlier))[0]


def mix_kernel(y_ref, core_ref, inputs, *refs):
    pieces, mixed, total = refs[:8], refs[8], refs[9]
    for side in range(2):
        for step in range(4):
            piece = pieces[4 * side + step]
            y_at = lax.rem(y_ref[0] + step, 4)
            core = core_ref[0] if side == 0 else 1 - core_ref[0]
            for x_high in range(2):
                row = (x_high * 8 + y_at * 2 + core) * OWN
                total[pl.ds(pl.multiple_of(row, 16), OWN), :] = piece[x_high, :OWN, :SEQ].astype(
                    jnp.float32
                )
    mixed[...] = (inputs[...].astype(jnp.float32) + total[...].T).astype(jnp.bfloat16)


def mix(y_at, core, inputs, pieces):
    smem = pl.BlockSpec(memory_space=pltpu.SMEM)
    vmem = pl.BlockSpec(memory_space=pltpu.VMEM)
    return pl.pallas_call(
        mix_kernel,
        in_specs=[smem, smem] + [vmem] * 9,
        out_shape=jax.ShapeDtypeStruct((SEQ, D), jnp.bfloat16),
        scratch_shapes=[pltpu.VMEM((D, SEQ), jnp.float32)],
        compiler_params=pltpu.CompilerParams(vmem_limit_bytes=24 * 2**20),
    )(y_at, core, inputs, *pieces)


def shards(inputs, norm_gain, w_gate, w_up, w_down, feat_dirs, unit_dirs, cotangent, lengths):
    t_index = lax.axis_index("tensor")
    d_index = lax.axis_index("dp")
    core = t_index % 2
    y_at = (t_index // 2) % 4
    x_high = t_index // 8
    core_index = core.astype(jnp.int32)[None]
    rows = inputs.reshape(SEQ, D)
    gain = norm_gain.reshape(D // 128, 128)
    normed, masked, mine, inverse = own_rows(
        core_index, lengths, rows, gain, cotangent.reshape(SEQ, D)
    )

    from_pair = move(mine, to_pair)
    from_down = move(mine, to_up)
    from_up = move(mine, to_down)

    first_column = d_index * SLICE
    window_start = (first_column // 128 * 128).astype(jnp.int32)[None]
    window_offset = (first_column % 128).astype(jnp.int32)[None]
    *own, kept, sent, own_normed_cut, own_cot_cut, own_cot = own_work(
        window_start, t_index.astype(jnp.int32)[None], normed, masked, rows, inverse,
        gain, w_gate, w_up, w_down, feat_dirs, unit_dirs,
    )
    own = (*own, own_normed_cut, own_cot_cut)

    from_pair, from_down, from_up, kept, sent = after(
        (from_pair, from_down, from_up, kept, sent), own
    )
    kept_sibling = move(sent, to_sibling)
    x_second = move(from_down, to_pair)
    up_second = move(from_down, to_up)
    down_second = move(from_pair, to_down)
    first_sources = [(a, move(a, to_sibling)) for a in (from_pair, from_down, from_up)]
    kept = kept.astype(jnp.float32) + kept_sibling.astype(jnp.float32)
    kept = kept.astype(jnp.bfloat16).reshape(4, 2, ROWS, LANES)
    arrived = [move(pick(kept, (y_at + step) % 4), along_y(step)) for step in (2, 1)]
    last_piece = pick(kept, (y_at + 3) % 4)
    total = pick(kept, y_at)

    def group_of(sources, owners):
        pieces = []
        flat = []
        for at, (pair, owner) in enumerate(zip(sources, owners)):
            for which in range(2):
                for item in range(pair[0].shape[0]):
                    pieces.append((2 * at + which, item, 48))
                    flat.append((owner, 48))
        arrays = [a for pair in sources for a in pair]
        worked = unit_work(window_start, arrays, tuple(pieces), w_gate, w_up, w_down)
        return worked, tuple(flat)

    first_sources = after(first_sources, total)
    first, owners_first = group_of(first_sources, (1, 2, 4))

    arrived, total, last_piece, x_second, up_second, down_second = after(
        (arrived, total, last_piece, x_second, up_second, down_second), first
    )
    arrived.append(move(last_piece, along_y(3)))
    third = [move(x_second, to_up)]
    second_sources = [(a, move(a, to_sibling)) for a in (x_second, up_second, down_second)]
    total = sum((a.astype(jnp.float32) for a in arrived), total.astype(jnp.float32))
    total = total.astype(jnp.bfloat16)
    total_far = move(total, to_far)

    second, owners_second = group_of(second_sources, (3, 6, 5))

    total, total_far, third = after((total, total_far, third), second)
    third_sources = [(a, move(a, to_sibling)) for a in third]
    total = total.astype(jnp.float32) + total_far.astype(jnp.float32)
    loss_dot = total[:1, 2 * OWN, :K]
    bound = 0.5 * math.sqrt(SEQ * D * FF)
    own_ratio = jnp.sqrt(jnp.mean(loss_dot * loss_dot, axis=1)) / bound
    scale = 1.0 / (N_DP * jnp.maximum(own_ratio, 1.0))
    scale_row = jnp.broadcast_to(scale[None, :], (1, 128))
    scale_pair = move(scale_row, to_pair)
    branch = total[:, OWN:].astype(jnp.bfloat16)
    branches = [branch] + [move(branch, along_y(-step)) for step in (1, 2, 3)]

    third, owners_third = group_of(third_sources, (7,))

    scale_pair, branches = after((scale_pair, branches), third)
    two = jnp.concatenate([scale_row, scale_pair], axis=0)
    two_down = move(two, along_z(1))
    two_up = move(two, along_z(-1))
    two_far = move(two, along_z(2))
    siblings = [move(a, to_sibling) for a in branches]
    own_back = pick(total, x_high)[:OWN, :SEQ]
    grad_input = ((own_back + own_cot) * scale).astype(jnp.bfloat16).T.reshape(1, SEQ, OWN)

    scales = jnp.concatenate([two[:, 0], two_down[:, 0], two_up[:, 0], two_far[:, 0]])
    grads = grad_work(
        window_offset,
        scales,
        (own, first, second, third),
        (((0, SEQ),), owners_first, owners_second, owners_third),
    )
    branches, siblings = after((branches, siblings), grads)
    mixed = mix(
        y_at.astype(jnp.int32)[None], core_index, rows, branches + siblings
    ).reshape(1, SEQ, D)
    every_loss = jnp.stack([a[0, OWN, :K] for a in branches + siblings])
    shared_loss = pick(every_loss, (4 - y_at) % 4 + 4 * core).astype(jnp.float32)[None, :]
    norm_ratio = jnp.sqrt(jnp.mean(shared_loss * shared_loss, axis=1)) / bound
    return (mixed, norm_ratio, grad_input, grads[0], grads[1], grads[2].T)


def solution(mesh):
    placed = (
        P("dp", None, None),
        P(),
        P(None, "tensor"),
        P(None, "tensor"),
        P("tensor", None),
        P(),
        P(None, None, "tensor"),
        P("dp", None, None),
        P("dp"),
    )
    return jax.shard_map(
        shards,
        mesh=mesh,
        in_specs=placed,
        out_specs=(
            P("dp", None, None),
            P("dp"),
            P("dp", None, "tensor"),
            P("dp", "tensor"),
            P("dp", "tensor"),
            P("tensor", "dp"),
        ),
        check_vma=False,
    )
```

```python
import functools
import math

import jax
import jax.numpy as jnp
from jax import lax
from jax.experimental import pallas as pl
from jax.experimental.pallas import tpu as pltpu
from jax.sharding import PartitionSpec as P

D = 2304
FF = 18432
SEQ = 192
K = 8
N_DP = 8
N_T = 16
UNITS = FF // N_T
SLICE = D // N_DP
OWN = D // N_T
BOTH = ("dp", "tensor")
TILE = 256
WINDOW = 384
LANES = 256
ROWS = 2 * OWN + 16


def device_index(x, y, z, core):
    x, y, z = x % 4, y % 4, z % 4
    return ((x % 2) * 4 + z) * N_T + ((x // 2) * 4 + y) * 2 + core


def move(array, target):
    pairs = [
        (device_index(x, y, z, core), device_index(*target(x, y, z, core)))
        for x in range(4)
        for y in range(4)
        for z in range(4)
        for core in range(2)
    ]
    return lax.ppermute(array, BOTH, pairs)


def to_pair(x, y, z, core):
    return (x ^ 1, y, z, core)


def to_up(x, y, z, core):
    return (x, y, z + 1, core)


def to_down(x, y, z, core):
    return (x, y, z - 1, core)


def to_sibling(x, y, z, core):
    return (x, y, z, 1 - core)


def to_far(x, y, z, core):
    return (x ^ 2, y, z, core)


def along_y(step):
    return lambda x, y, z, core: (x, y + step, z, core)


def along_z(step):
    return lambda x, y, z, core: (x, y, z + step, core)


def gelu_pair(value):
    coef = math.sqrt(2.0 / math.pi)
    tangent = jnp.tanh(coef * (value + 0.044715 * value * value * value))
    activated = 0.5 * value * (1.0 + tangent)
    slope = 0.5 * (1.0 + tangent) + 0.5 * value * (1.0 - tangent * tangent) * coef * (
        1.0 + 3.0 * 0.044715 * value * value
    )
    return (activated, slope)


def contract_last(left, right):
    return lax.dot_general(
        left, right, (((1,), (1,)), ((), ())), preferred_element_type=jnp.float32
    )


def contract_first(left, right):
    return lax.dot_general(
        left, right, (((0,), (0,)), ((), ())), preferred_element_type=jnp.float32
    )


def as_row(ref):
    return jnp.concatenate([ref[at : at + 1, :] for at in range(D // 128)], axis=1)


def rows_kernel(core_ref, length_ref, inputs, gain, cot, normed, masked, mine, inverse):
    wide = inputs[...].astype(jnp.float32)
    inv = lax.rsqrt(jnp.mean(wide * wide, axis=-1, keepdims=True) + 1e-06)
    inverse[...] = inv
    normed[...] = (wide * inv * as_row(gain)).astype(jnp.bfloat16)
    valid = lax.broadcasted_iota(jnp.int32, (SEQ, 1), 0) < length_ref[0]
    masked[...] = (cot[...].astype(jnp.float32) * valid.astype(jnp.float32)).astype(jnp.bfloat16)
    for half in range(2):
        rows = pl.ds(pl.multiple_of(core_ref[0] * 96 + half * 48, 16), 48)
        mine[half, 0] = normed[rows, :]
        mine[half, 1] = masked[rows, :]


def own_rows(core, lengths, inputs, gain, cot):
    smem = pl.BlockSpec(memory_space=pltpu.SMEM)
    vmem = pl.BlockSpec(memory_space=pltpu.VMEM)
    return pl.pallas_call(
        rows_kernel,
        in_specs=[smem, smem, vmem, vmem, vmem],
        out_shape=[
            jax.ShapeDtypeStruct((SEQ, D), jnp.bfloat16),
            jax.ShapeDtypeStruct((SEQ, D), jnp.bfloat16),
            jax.ShapeDtypeStruct((2, 2, 48, D), jnp.bfloat16),
            jax.ShapeDtypeStruct((SEQ, 1), jnp.float32),
        ],
        compiler_params=pltpu.CompilerParams(vmem_limit_bytes=58 * 2**20),
    )(core, lengths, inputs, gain, cot)


def own_kernel(
    start_ref, own_ref, normed, masked, inputs, inverse, gain, gate_hbm, up_hbm, down_hbm, feats,
    units, hidden, dgate, dup, kept, sent, normed_cut, cot_cut, own_cot,
    gate_w, up_w, down_w, gate, up_proj, branch, dnormed, turned, sems,
):
    loads = [
        pltpu.make_async_copy(source, into, sems.at[at])
        for at, (source, into) in enumerate(
            ((gate_hbm, gate_w), (up_hbm, up_w), (down_hbm, down_w))
        )
    ]
    for load in loads:
        load.start()
    window = pl.ds(pl.multiple_of(start_ref[0], 128), WINDOW)
    normed_cut[...] = normed[:, window]
    cot_cut[...] = masked[:, window]
    turned[...] = masked[...].astype(jnp.float32).T
    own_cot[...] = turned[pl.ds(pl.multiple_of(own_ref[0] * OWN, 16), OWN), :]

    def split_dirs(dirs):
        high = dirs.astype(jnp.bfloat16).astype(jnp.float32)
        return jnp.concatenate([high, dirs - high]).astype(jnp.bfloat16)

    def onto(array, dirs):
        both = contract_last(array[...], split_dirs(dirs))
        return both[:, :K] + both[:, K:]

    tiles = [slice(at, min(at + TILE, UNITS)) for at in range(0, UNITS, TILE)]
    wide_tiles = [slice(at, at + 768) for at in range(0, D, 768)]
    loads[0].wait()
    for tile in tiles:
        gate[:, tile] = jnp.dot(normed[...], gate_w[:, tile], preferred_element_type=jnp.float32)
    loads[1].wait()
    for tile in tiles:
        up_proj[:, tile] = jnp.dot(normed[...], up_w[:, tile], preferred_element_type=jnp.float32)
    loads[2].wait()
    for tile in tiles:
        dhidden = contract_last(masked[...], down_w[tile, :])
        activated, slope = gelu_pair(gate[:, tile])
        up_tile = up_proj[:, tile]
        hidden[:, tile] = (activated * up_tile).astype(jnp.bfloat16)
        dgate[:, tile] = (dhidden * up_tile * slope).astype(jnp.bfloat16)
        dup[:, tile] = (dhidden * activated).astype(jnp.bfloat16)
    for tile in wide_tiles:
        branch[:, tile] = jnp.dot(hidden[...], down_w[:, tile], preferred_element_type=jnp.float32)
    for tile in wide_tiles:
        dnormed[:, tile] = contract_last(dgate[...], gate_w[tile, :]) + contract_last(
            dup[...], up_w[tile, :]
        )
    loss = jnp.sum(
        onto(dgate, units[0]) * onto(normed, feats[0])
        + onto(dup, units[1]) * onto(normed, feats[1])
        + onto(hidden, units[2]) * onto(masked, feats[2]),
        axis=0,
        keepdims=True,
    )
    wide = inputs[...].astype(jnp.float32)
    inv = inverse[...]
    gained = dnormed[...] * as_row(gain)
    back = gained * inv - wide * (inv * inv * inv) * jnp.mean(
        gained * wide, axis=-1, keepdims=True
    )
    branch_t = branch[...].T.astype(jnp.bfloat16)
    back_t = back.T.astype(jnp.bfloat16)
    loss_rows = jnp.broadcast_to(loss, (16, K)).astype(jnp.bfloat16)
    first_core = lax.rem(own_ref[0], 2) == 0
    for place in range(8):
        t = place % 2 * 8 + place // 2 * 2
        for into, low_first in ((kept, first_core), (sent, jnp.logical_not(first_core))):
            for at, array in enumerate((back_t, branch_t)):
                into[place, at * OWN : (at + 1) * OWN, :SEQ] = jnp.where(
                    low_first,
                    array[t * OWN : (t + 1) * OWN],
                    array[(t + 1) * OWN : (t + 2) * OWN],
                )
            into[place, :, SEQ:] = jnp.zeros((ROWS, LANES - SEQ), jnp.bfloat16)
            into[place, 2 * OWN :, :SEQ] = jnp.zeros((16, SEQ), jnp.bfloat16)
            into[place, 2 * OWN :, :K] = loss_rows


def own_work(start, own_at, normed, masked, inputs, inverse, gain, w_gate, w_up, w_down, feats, units):
    smem = pl.BlockSpec(memory_space=pltpu.SMEM)
    vmem = pl.BlockSpec(memory_space=pltpu.VMEM)
    far = pl.BlockSpec(memory_space=pl.ANY)
    return pl.pallas_call(
        own_kernel,
        in_specs=[smem] * 2 + [vmem] * 5 + [far] * 3 + [vmem] * 2,
        out_shape=[jax.ShapeDtypeStruct((SEQ, UNITS), jnp.bfloat16)] * 3
        + [jax.ShapeDtypeStruct((8, ROWS, LANES), jnp.bfloat16)] * 2
        + [jax.ShapeDtypeStruct((SEQ, WINDOW), jnp.bfloat16)] * 2
        + [jax.ShapeDtypeStruct((OWN, SEQ), jnp.float32)],
        scratch_shapes=[
            pltpu.VMEM((D, UNITS), jnp.bfloat16),
            pltpu.VMEM((D, UNITS), jnp.bfloat16),
            pltpu.VMEM((UNITS, D), jnp.bfloat16),
            pltpu.VMEM((SEQ, UNITS), jnp.float32),
            pltpu.VMEM((SEQ, UNITS), jnp.float32),
            pltpu.VMEM((SEQ, D), jnp.float32),
            pltpu.VMEM((SEQ, D), jnp.float32),
            pltpu.VMEM((D, SEQ), jnp.float32),
            pltpu.SemaphoreType.DMA((3,)),
        ],
        compiler_params=pltpu.CompilerParams(vmem_limit_bytes=58 * 2**20),
        cost_estimate=pl.CostEstimate(
            flops=10 * SEQ * D * UNITS, bytes_accessed=7 * D * UNITS, transcendentals=SEQ * UNITS
        ),
    )(start, own_at, normed, masked, inputs, inverse, gain, w_gate, w_up, w_down, feats, units)


def unit_kernel(pieces, count, start_ref, *refs):
    sources, refs = refs[:count], refs[count:]
    weights, outs, cuts, refs = refs[:3], refs[3:6], refs[6:8], refs[8:]
    normed, cot, gate_w, up_w, down_w, gate, up_proj, hidden, dgate, dup = refs[:10]
    sems, weight_sems, out_sems = refs[10:]
    row_copies = ([], [])
    row = 0
    for at, (src, item, size) in enumerate(pieces):
        for which, into in enumerate((normed, cot)):
            row_copies[which].append(
                pltpu.make_async_copy(
                    sources[src].at[item, which],
                    into.at[pl.ds(row, size)],
                    sems.at[2 * at + which],
                )
            )
        row += size
    loads = [
        pltpu.make_async_copy(weight, into, weight_sems.at[at])
        for at, (weight, into) in enumerate(zip(weights, (gate_w, up_w, down_w)))
    ]
    later = loads[1:2] + row_copies[1] + loads[2:]
    for copy in row_copies[0] + loads[:1] + (later if row <= SEQ else []):
        copy.start()
    window = pl.ds(pl.multiple_of(start_ref[0], 128), WINDOW)
    tiles = [slice(at, min(at + TILE, UNITS)) for at in range(0, UNITS, TILE)]
    for copy in row_copies[0] + loads[:1]:
        copy.wait()
    if row > SEQ:
        for copy in later:
            copy.start()
    for tile in tiles:
        gate[:, tile] = jnp.dot(normed[...], gate_w[:, tile], preferred_element_type=jnp.float32)
    cuts[0][...] = normed[:, window]
    loads[1].wait()
    for tile in tiles:
        up_proj[:, tile] = jnp.dot(normed[...], up_w[:, tile], preferred_element_type=jnp.float32)
    for copy in row_copies[1] + loads[2:]:
        copy.wait()
    cuts[1][...] = cot[:, window]
    stores = []
    for tile in tiles:
        dhidden = contract_last(cot[...], down_w[tile, :])
        activated, slope = gelu_pair(gate[:, tile])
        up_tile = up_proj[:, tile]
        hidden[:, tile] = (activated * up_tile).astype(jnp.bfloat16)
        dgate[:, tile] = (dhidden * up_tile * slope).astype(jnp.bfloat16)
        dup[:, tile] = (dhidden * activated).astype(jnp.bfloat16)
        for source, into in zip((hidden, dgate, dup), outs):
            store = pltpu.make_async_copy(
                source.at[:, tile], into.at[:, tile], out_sems.at[len(stores)]
            )
            store.start()
            stores.append(store)
    for store in stores:
        store.wait()


def unit_work(start, sources, pieces, w_gate, w_up, w_down):
    rows = sum(piece[2] for piece in pieces)
    far = pl.BlockSpec(memory_space=pl.ANY)
    vmem = pl.BlockSpec(memory_space=pltpu.VMEM)
    by_unit = pltpu.VMEM((rows, UNITS), jnp.bfloat16)
    return pl.pallas_call(
        functools.partial(unit_kernel, pieces, len(sources)),
        in_specs=[pl.BlockSpec(memory_space=pltpu.SMEM)] + [far] * (len(sources) + 3),
        out_specs=[far] * 3 + [vmem] * 2,
        out_shape=[jax.ShapeDtypeStruct((rows, UNITS), jnp.bfloat16)] * 3
        + [jax.ShapeDtypeStruct((rows, WINDOW), jnp.bfloat16)] * 2,
        scratch_shapes=[
            pltpu.VMEM((rows, D), jnp.bfloat16),
            pltpu.VMEM((rows, D), jnp.bfloat16),
            pltpu.VMEM((D, UNITS), jnp.bfloat16),
            pltpu.VMEM((D, UNITS), jnp.bfloat16),
            pltpu.VMEM((UNITS, D), jnp.bfloat16),
            pltpu.VMEM((rows, UNITS), jnp.float32),
            pltpu.VMEM((rows, UNITS), jnp.float32),
            by_unit,
            by_unit,
            by_unit,
            pltpu.SemaphoreType.DMA((2 * len(pieces),)),
            pltpu.SemaphoreType.DMA((3,)),
            pltpu.SemaphoreType.DMA((3 * -(-UNITS // TILE),)),
        ],
        compiler_params=pltpu.CompilerParams(vmem_limit_bytes=58 * 2**20),
        cost_estimate=pl.CostEstimate(
            flops=6 * rows * D * UNITS,
            bytes_accessed=6 * D * UNITS + 4 * rows * D + 6 * rows * UNITS,
            transcendentals=rows * UNITS,
        ),
    )(start, *sources, w_gate, w_up, w_down)


def grad_kernel(owners, sizes, offset_ref, scale_ref, *refs):
    groups, refs = refs[: 5 * len(sizes)], refs[5 * len(sizes) :]
    outs, (hidden, dgate, dup, left, right, wide, sems) = refs[:3], refs[3:]
    copies = {}
    for which, into in ((1, dgate), (2, dup), (0, hidden)):
        row = 0
        for at, size in enumerate(sizes):
            copy = pltpu.make_async_copy(
                groups[5 * at + which], into.at[pl.ds(row, size)], sems.at[3 * at + which]
            )
            copies[which, at] = copy
            row += size
            if which == 1:
                copy.start()
    row = 0
    for at in range(len(sizes)):
        inside = 0
        for owner, size in owners[at]:
            scale = scale_ref[owner]
            here, there = pl.ds(inside, size), pl.ds(row, size)
            for side, into in ((3, left), (4, right)):
                into[there, :] = (
                    groups[5 * at + side][here, :].astype(jnp.float32) * scale
                ).astype(jnp.bfloat16)
            inside += size
            row += size
    offset = pl.multiple_of(offset_ref[0], 32)
    place = 0
    for which, factor, array, out in (
        (1, left, dgate, outs[0]),
        (2, left, dup, outs[1]),
        (0, right, hidden, outs[2]),
    ):
        for at in range(len(sizes)):
            copies[which, at].wait()
        if which == 1:
            for later in (2, 0):
                for at in range(len(sizes)):
                    copies[later, at].start()
        for start in range(0, UNITS, TILE):
            tile = slice(start, min(start + TILE, UNITS))
            columns = slice(0, tile.stop - tile.start)
            wide[place % 3, :, columns] = contract_first(factor[...], array[:, tile])
            out[:, tile] = wide[place % 3, pl.ds(offset, SLICE), columns].astype(jnp.bfloat16)
            place += 1


def grad_work(offset, scales, groups, owners):
    sizes = [group[0].shape[0] for group in groups]
    rows = sum(sizes)
    far = pl.BlockSpec(memory_space=pl.ANY)
    vmem = pl.BlockSpec(memory_space=pltpu.VMEM)
    return pl.pallas_call(
        functools.partial(grad_kernel, owners, sizes),
        in_specs=[pl.BlockSpec(memory_space=pltpu.SMEM)] * 2
        + ([far] * 3 + [vmem] * 2) * len(sizes),
        out_shape=[jax.ShapeDtypeStruct((SLICE, UNITS), jnp.bfloat16)] * 3,
        scratch_shapes=[
            pltpu.VMEM((rows, UNITS), jnp.bfloat16),
            pltpu.VMEM((rows, UNITS), jnp.bfloat16),
            pltpu.VMEM((rows, UNITS), jnp.bfloat16),
            pltpu.VMEM((rows, WINDOW), jnp.bfloat16),
            pltpu.VMEM((rows, WINDOW), jnp.bfloat16),
            pltpu.VMEM((3, WINDOW, TILE), jnp.float32),
            pltpu.SemaphoreType.DMA((3 * len(sizes),)),
        ],
        compiler_params=pltpu.CompilerParams(vmem_limit_bytes=58 * 2**20),
        cost_estimate=pl.CostEstimate(
            flops=6 * rows * WINDOW * UNITS,
            bytes_accessed=6 * rows * UNITS + 6 * SLICE * UNITS + 4 * rows * WINDOW,
            transcendentals=0,
        ),
    )(offset, scales, *[array for group in groups for array in group])


def pick(array, index):
    return lax.dynamic_index_in_dim(array, index, 0, keepdims=False)


def after(arrays, *earlier):
    return lax.optimization_barrier((arrays, earlier))[0]


def mix_kernel(y_ref, core_ref, inputs, *refs):
    pieces, mixed, total = refs[:8], refs[8], refs[9]
    for side in range(2):
        for step in range(4):
            piece = pieces[4 * side + step]
            y_at = lax.rem(y_ref[0] + step, 4)
            core = core_ref[0] if side == 0 else 1 - core_ref[0]
            for x_high in range(2):
                row = (x_high * 8 + y_at * 2 + core) * OWN
                total[pl.ds(pl.multiple_of(row, 16), OWN), :] = piece[x_high, :OWN, :SEQ].astype(
                    jnp.float32
                )
    mixed[...] = (inputs[...].astype(jnp.float32) + total[...].T).astype(jnp.bfloat16)


def mix(y_at, core, inputs, pieces):
    smem = pl.BlockSpec(memory_space=pltpu.SMEM)
    vmem = pl.BlockSpec(memory_space=pltpu.VMEM)
    return pl.pallas_call(
        mix_kernel,
        in_specs=[smem, smem] + [vmem] * 9,
        out_shape=jax.ShapeDtypeStruct((SEQ, D), jnp.bfloat16),
        scratch_shapes=[pltpu.VMEM((D, SEQ), jnp.float32)],
        compiler_params=pltpu.CompilerParams(vmem_limit_bytes=24 * 2**20),
    )(y_at, core, inputs, *pieces)


def shards(inputs, norm_gain, w_gate, w_up, w_down, feat_dirs, unit_dirs, cotangent, lengths):
    t_index = lax.axis_index("tensor")
    d_index = lax.axis_index("dp")
    core = t_index % 2
    y_at = (t_index // 2) % 4
    x_high = t_index // 8
    core_index = core.astype(jnp.int32)[None]
    rows = inputs.reshape(SEQ, D)
    gain = norm_gain.reshape(D // 128, 128)
    normed, masked, mine, inverse = own_rows(
        core_index, lengths, rows, gain, cotangent.reshape(SEQ, D)
    )

    from_pair = move(mine, to_pair)
    from_down = move(mine, to_up)
    from_up = move(mine, to_down)

    first_column = d_index * SLICE
    window_start = (first_column // 128 * 128).astype(jnp.int32)[None]
    window_offset = (first_column % 128).astype(jnp.int32)[None]
    *own, kept, sent, own_normed_cut, own_cot_cut, own_cot = own_work(
        window_start, t_index.astype(jnp.int32)[None], normed, masked, rows, inverse,
        gain, w_gate, w_up, w_down, feat_dirs, unit_dirs,
    )
    own = (*own, own_normed_cut, own_cot_cut)

    from_pair, from_down, from_up, kept, sent = after(
        (from_pair, from_down, from_up, kept, sent), own
    )
    kept_sibling = move(sent, to_sibling)
    x_second = move(from_down, to_pair)
    up_second = move(from_down, to_up)
    first_sources = [(a, move(a, to_sibling)) for a in (from_pair, from_down, from_up)]
    kept = kept.astype(jnp.float32) + kept_sibling.astype(jnp.float32)
    kept = kept.astype(jnp.bfloat16).reshape(4, 2, ROWS, LANES)
    arrived = [move(pick(kept, (y_at + step) % 4), along_y(step)) for step in (2, 1, 3)]
    total = pick(kept, y_at)

    def group_of(sources, owners):
        pieces = []
        flat = []
        for at, (pair, owner) in enumerate(zip(sources, owners)):
            for which in range(2):
                for item in range(pair[0].shape[0]):
                    pieces.append((2 * at + which, item, 48))
                    flat.append((owner, 48))
        arrays = [a for pair in sources for a in pair]
        worked = unit_work(window_start, arrays, tuple(pieces), w_gate, w_up, w_down)
        return worked, tuple(flat)

    first_sources = after(first_sources, total)
    first, owners_first = group_of(first_sources, (1, 2, 4))

    arrived, total, x_second, up_second, from_pair = after(
        (arrived, total, x_second, up_second, from_pair), first
    )
    third = [move(from_pair, to_down), move(x_second, to_up)]
    second_sources = [(a, move(a, to_sibling)) for a in (x_second, up_second)]
    total = sum((a.astype(jnp.float32) for a in arrived), total.astype(jnp.float32))
    total = total.astype(jnp.bfloat16)
    total_far = move(total, to_far)

    second, owners_second = group_of(second_sources, (3, 6))

    total, total_far, third = after((total, total_far, third), second)
    third_sources = [(a, move(a, to_sibling)) for a in third]
    total = total.astype(jnp.float32) + total_far.astype(jnp.float32)
    loss_dot = total[:1, 2 * OWN, :K]
    bound = 0.5 * math.sqrt(SEQ * D * FF)
    own_ratio = jnp.sqrt(jnp.mean(loss_dot * loss_dot, axis=1)) / bound
    scale = 1.0 / (N_DP * jnp.maximum(own_ratio, 1.0))
    scale_row = jnp.broadcast_to(scale[None, :], (1, 128))
    scale_pair = move(scale_row, to_pair)
    branch = total[:, OWN:].astype(jnp.bfloat16)
    branches = [branch] + [move(branch, along_y(-step)) for step in (1, 2, 3)]

    third, owners_third = group_of(third_sources, (5, 7))

    scale_pair, branches = after((scale_pair, branches), third)
    two = jnp.concatenate([scale_row, scale_pair], axis=0)
    two_down = move(two, along_z(1))
    two_up = move(two, along_z(-1))
    two_far = move(two, along_z(2))
    siblings = [move(a, to_sibling) for a in branches]
    own_back = pick(total, x_high)[:OWN, :SEQ]
    grad_input = ((own_back + own_cot) * scale).astype(jnp.bfloat16).T.reshape(1, SEQ, OWN)

    scales = jnp.concatenate([two[:, 0], two_down[:, 0], two_up[:, 0], two_far[:, 0]])
    grads = grad_work(
        window_offset,
        scales,
        (own, first, second, third),
        (((0, SEQ),), owners_first, owners_second, owners_third),
    )
    branches, siblings = after((branches, siblings), grads)
    mixed = mix(
        y_at.astype(jnp.int32)[None], core_index, rows, branches + siblings
    ).reshape(1, SEQ, D)
    every_loss = jnp.stack([a[0, OWN, :K] for a in branches + siblings])
    shared_loss = pick(every_loss, (4 - y_at) % 4 + 4 * core).astype(jnp.float32)[None, :]
    norm_ratio = jnp.sqrt(jnp.mean(shared_loss * shared_loss, axis=1)) / bound
    return (mixed, norm_ratio, grad_input, grads[0], grads[1], grads[2].T)


def solution(mesh):
    placed = (
        P("dp", None, None),
        P(),
        P(None, "tensor"),
        P(None, "tensor"),
        P("tensor", None),
        P(),
        P(None, None, "tensor"),
        P("dp", None, None),
        P("dp"),
    )
    return jax.shard_map(
        shards,
        mesh=mesh,
        in_specs=placed,
        out_specs=(
            P("dp", None, None),
            P("dp"),
            P("dp", None, "tensor"),
            P("dp", "tensor"),
            P("dp", "tensor"),
            P("tensor", "dp"),
        ),
        check_vma=False,
    )
```

```python
import functools
import math

import jax
import jax.numpy as jnp
from jax import lax
from jax.experimental import pallas as pl
from jax.experimental.pallas import tpu as pltpu
from jax.sharding import PartitionSpec as P

D = 2304
FF = 18432
SEQ = 192
K = 8
N_DP = 8
N_T = 16
UNITS = FF // N_T
SLICE = D // N_DP
OWN = D // N_T
BOTH = ("dp", "tensor")
TILE = 512
WINDOW = 384
LANES = 256
ROWS = 2 * OWN + 16


def device_index(x, y, z, core):
    x, y, z = x % 4, y % 4, z % 4
    return ((x % 2) * 4 + z) * N_T + ((x // 2) * 4 + y) * 2 + core


def move(array, target):
    pairs = [
        (device_index(x, y, z, core), device_index(*target(x, y, z, core)))
        for x in range(4)
        for y in range(4)
        for z in range(4)
        for core in range(2)
    ]
    return lax.ppermute(array, BOTH, pairs)


def to_pair(x, y, z, core):
    return (x ^ 1, y, z, core)


def to_up(x, y, z, core):
    return (x, y, z + 1, core)


def to_down(x, y, z, core):
    return (x, y, z - 1, core)


def to_sibling(x, y, z, core):
    return (x, y, z, 1 - core)


def to_far(x, y, z, core):
    return (x ^ 2, y, z, core)


def along_y(step):
    return lambda x, y, z, core: (x, y + step, z, core)


def along_z(step):
    return lambda x, y, z, core: (x, y, z + step, core)


def gelu_pair(value):
    coef = math.sqrt(2.0 / math.pi)
    tangent = jnp.tanh(coef * (value + 0.044715 * value * value * value))
    activated = 0.5 * value * (1.0 + tangent)
    slope = 0.5 * (1.0 + tangent) + 0.5 * value * (1.0 - tangent * tangent) * coef * (
        1.0 + 3.0 * 0.044715 * value * value
    )
    return (activated, slope)


def contract_last(left, right):
    return lax.dot_general(
        left, right, (((1,), (1,)), ((), ())), preferred_element_type=jnp.float32
    )


def contract_first(left, right):
    return lax.dot_general(
        left, right, (((0,), (0,)), ((), ())), preferred_element_type=jnp.float32
    )


def as_row(ref):
    return jnp.concatenate([ref[at : at + 1, :] for at in range(D // 128)], axis=1)


def rows_kernel(core_ref, length_ref, inputs, gain, cot, normed, masked, mine, inverse):
    wide = inputs[...].astype(jnp.float32)
    inv = lax.rsqrt(jnp.mean(wide * wide, axis=-1, keepdims=True) + 1e-06)
    inverse[...] = inv
    normed[...] = (wide * inv * as_row(gain)).astype(jnp.bfloat16)
    valid = lax.broadcasted_iota(jnp.int32, (SEQ, 1), 0) < length_ref[0]
    masked[...] = (cot[...].astype(jnp.float32) * valid.astype(jnp.float32)).astype(jnp.bfloat16)
    for half in range(2):
        rows = pl.ds(pl.multiple_of(core_ref[0] * 96 + half * 48, 16), 48)
        mine[half, 0] = normed[rows, :]
        mine[half, 1] = masked[rows, :]


def own_rows(core, lengths, inputs, gain, cot):
    smem = pl.BlockSpec(memory_space=pltpu.SMEM)
    vmem = pl.BlockSpec(memory_space=pltpu.VMEM)
    return pl.pallas_call(
        rows_kernel,
        in_specs=[smem, smem, vmem, vmem, vmem],
        out_shape=[
            jax.ShapeDtypeStruct((SEQ, D), jnp.bfloat16),
            jax.ShapeDtypeStruct((SEQ, D), jnp.bfloat16),
            jax.ShapeDtypeStruct((2, 2, 48, D), jnp.bfloat16),
            jax.ShapeDtypeStruct((SEQ, 1), jnp.float32),
        ],
        compiler_params=pltpu.CompilerParams(vmem_limit_bytes=58 * 2**20),
    )(core, lengths, inputs, gain, cot)


def own_kernel(
    start_ref, own_ref, normed, masked, inputs, inverse, gain, gate_hbm, up_hbm, down_hbm, feats,
    units, hidden, dgate, dup, kept, sent, normed_cut, cot_cut, own_cot,
    gate_w, up_w, down_w, gate, up_proj, branch, dnormed, turned, sems,
):
    loads = [
        pltpu.make_async_copy(source, into, sems.at[at])
        for at, (source, into) in enumerate(
            ((gate_hbm, gate_w), (up_hbm, up_w), (down_hbm, down_w))
        )
    ]
    for load in loads:
        load.start()
    window = pl.ds(pl.multiple_of(start_ref[0], 128), WINDOW)
    normed_cut[...] = normed[:, window]
    cot_cut[...] = masked[:, window]
    turned[...] = masked[...].astype(jnp.float32).T
    own_cot[...] = turned[pl.ds(pl.multiple_of(own_ref[0] * OWN, 16), OWN), :]

    def split_dirs(dirs):
        high = dirs.astype(jnp.bfloat16).astype(jnp.float32)
        return jnp.concatenate([high, dirs - high]).astype(jnp.bfloat16)

    def onto(array, dirs):
        both = contract_last(array[...], split_dirs(dirs))
        return both[:, :K] + both[:, K:]

    tiles = [slice(at, min(at + TILE, UNITS)) for at in range(0, UNITS, TILE)]
    wide_tiles = [slice(at, at + 768) for at in range(0, D, 768)]
    loads[0].wait()
    for tile in tiles:
        gate[:, tile] = jnp.dot(normed[...], gate_w[:, tile], preferred_element_type=jnp.float32)
    loads[1].wait()
    for tile in tiles:
        up_proj[:, tile] = jnp.dot(normed[...], up_w[:, tile], preferred_element_type=jnp.float32)
    loads[2].wait()
    for tile in tiles:
        dhidden = contract_last(masked[...], down_w[tile, :])
        activated, slope = gelu_pair(gate[:, tile])
        up_tile = up_proj[:, tile]
        hidden[:, tile] = (activated * up_tile).astype(jnp.bfloat16)
        dgate[:, tile] = (dhidden * up_tile * slope).astype(jnp.bfloat16)
        dup[:, tile] = (dhidden * activated).astype(jnp.bfloat16)
    for tile in wide_tiles:
        branch[:, tile] = jnp.dot(hidden[...], down_w[:, tile], preferred_element_type=jnp.float32)
    for tile in wide_tiles:
        dnormed[:, tile] = contract_last(dgate[...], gate_w[tile, :]) + contract_last(
            dup[...], up_w[tile, :]
        )
    loss = jnp.sum(
        onto(dgate, units[0]) * onto(normed, feats[0])
        + onto(dup, units[1]) * onto(normed, feats[1])
        + onto(hidden, units[2]) * onto(masked, feats[2]),
        axis=0,
        keepdims=True,
    )
    wide = inputs[...].astype(jnp.float32)
    inv = inverse[...]
    gained = dnormed[...] * as_row(gain)
    back = gained * inv - wide * (inv * inv * inv) * jnp.mean(
        gained * wide, axis=-1, keepdims=True
    )
    branch_t = branch[...].T.astype(jnp.bfloat16)
    back_t = back.T.astype(jnp.bfloat16)
    loss_rows = jnp.broadcast_to(loss, (16, K)).astype(jnp.bfloat16)
    first_core = lax.rem(own_ref[0], 2) == 0
    for place in range(8):
        t = place % 2 * 8 + place // 2 * 2
        for into, low_first in ((kept, first_core), (sent, jnp.logical_not(first_core))):
            for at, array in enumerate((back_t, branch_t)):
                into[place, at * OWN : (at + 1) * OWN, :SEQ] = jnp.where(
                    low_first,
                    array[t * OWN : (t + 1) * OWN],
                    array[(t + 1) * OWN : (t + 2) * OWN],
                )
            into[place, :, SEQ:] = jnp.zeros((ROWS, LANES - SEQ), jnp.bfloat16)
            into[place, 2 * OWN :, :SEQ] = jnp.zeros((16, SEQ), jnp.bfloat16)
            into[place, 2 * OWN :, :K] = loss_rows


def own_work(start, own_at, normed, masked, inputs, inverse, gain, w_gate, w_up, w_down, feats, units):
    smem = pl.BlockSpec(memory_space=pltpu.SMEM)
    vmem = pl.BlockSpec(memory_space=pltpu.VMEM)
    far = pl.BlockSpec(memory_space=pl.ANY)
    return pl.pallas_call(
        own_kernel,
        in_specs=[smem] * 2 + [vmem] * 5 + [far] * 3 + [vmem] * 2,
        out_shape=[jax.ShapeDtypeStruct((SEQ, UNITS), jnp.bfloat16)] * 3
        + [jax.ShapeDtypeStruct((8, ROWS, LANES), jnp.bfloat16)] * 2
        + [jax.ShapeDtypeStruct((SEQ, WINDOW), jnp.bfloat16)] * 2
        + [jax.ShapeDtypeStruct((OWN, SEQ), jnp.float32)],
        scratch_shapes=[
            pltpu.VMEM((D, UNITS), jnp.bfloat16),
            pltpu.VMEM((D, UNITS), jnp.bfloat16),
            pltpu.VMEM((UNITS, D), jnp.bfloat16),
            pltpu.VMEM((SEQ, UNITS), jnp.float32),
            pltpu.VMEM((SEQ, UNITS), jnp.float32),
            pltpu.VMEM((SEQ, D), jnp.float32),
            pltpu.VMEM((SEQ, D), jnp.float32),
            pltpu.VMEM((D, SEQ), jnp.float32),
            pltpu.SemaphoreType.DMA((3,)),
        ],
        compiler_params=pltpu.CompilerParams(vmem_limit_bytes=58 * 2**20),
        cost_estimate=pl.CostEstimate(
            flops=10 * SEQ * D * UNITS, bytes_accessed=7 * D * UNITS, transcendentals=SEQ * UNITS
        ),
    )(start, own_at, normed, masked, inputs, inverse, gain, w_gate, w_up, w_down, feats, units)


def unit_kernel(pieces, count, start_ref, *refs):
    sources, refs = refs[:count], refs[count:]
    weights, outs, cuts, refs = refs[:3], refs[3:6], refs[6:8], refs[8:]
    normed, cot, gate_w, up_w, down_w, gate, up_proj, hidden, dgate, dup = refs[:10]
    sems, weight_sems, out_sems = refs[10:]
    row_copies = ([], [])
    row = 0
    for at, (src, item, size) in enumerate(pieces):
        for which, into in enumerate((normed, cot)):
            row_copies[which].append(
                pltpu.make_async_copy(
                    sources[src].at[item, which],
                    into.at[pl.ds(row, size)],
                    sems.at[2 * at + which],
                )
            )
        row += size
    loads = [
        pltpu.make_async_copy(weight, into, weight_sems.at[at])
        for at, (weight, into) in enumerate(zip(weights, (gate_w, up_w, down_w)))
    ]
    later = loads[1:2] + row_copies[1] + loads[2:]
    for copy in row_copies[0] + loads[:1] + (later if row <= SEQ else []):
        copy.start()
    window = pl.ds(pl.multiple_of(start_ref[0], 128), WINDOW)
    tiles = [slice(at, min(at + TILE, UNITS)) for at in range(0, UNITS, TILE)]
    for copy in row_copies[0] + loads[:1]:
        copy.wait()
    if row > SEQ:
        for copy in later:
            copy.start()
    for tile in tiles:
        gate[:, tile] = jnp.dot(normed[...], gate_w[:, tile], preferred_element_type=jnp.float32)
    cuts[0][...] = normed[:, window]
    loads[1].wait()
    for tile in tiles:
        up_proj[:, tile] = jnp.dot(normed[...], up_w[:, tile], preferred_element_type=jnp.float32)
    for copy in row_copies[1] + loads[2:]:
        copy.wait()
    cuts[1][...] = cot[:, window]
    stores = []
    for tile in tiles:
        dhidden = contract_last(cot[...], down_w[tile, :])
        activated, slope = gelu_pair(gate[:, tile])
        up_tile = up_proj[:, tile]
        hidden[:, tile] = (activated * up_tile).astype(jnp.bfloat16)
        dgate[:, tile] = (dhidden * up_tile * slope).astype(jnp.bfloat16)
        dup[:, tile] = (dhidden * activated).astype(jnp.bfloat16)
        for source, into in zip((hidden, dgate, dup), outs):
            store = pltpu.make_async_copy(
                source.at[:, tile], into.at[:, tile], out_sems.at[len(stores)]
            )
            store.start()
            stores.append(store)
    for store in stores:
        store.wait()


def unit_work(start, sources, pieces, w_gate, w_up, w_down):
    rows = sum(piece[2] for piece in pieces)
    far = pl.BlockSpec(memory_space=pl.ANY)
    vmem = pl.BlockSpec(memory_space=pltpu.VMEM)
    by_unit = pltpu.VMEM((rows, UNITS), jnp.bfloat16)
    return pl.pallas_call(
        functools.partial(unit_kernel, pieces, len(sources)),
        in_specs=[pl.BlockSpec(memory_space=pltpu.SMEM)] + [far] * (len(sources) + 3),
        out_specs=[far] * 3 + [vmem] * 2,
        out_shape=[jax.ShapeDtypeStruct((rows, UNITS), jnp.bfloat16)] * 3
        + [jax.ShapeDtypeStruct((rows, WINDOW), jnp.bfloat16)] * 2,
        scratch_shapes=[
            pltpu.VMEM((rows, D), jnp.bfloat16),
            pltpu.VMEM((rows, D), jnp.bfloat16),
            pltpu.VMEM((D, UNITS), jnp.bfloat16),
            pltpu.VMEM((D, UNITS), jnp.bfloat16),
            pltpu.VMEM((UNITS, D), jnp.bfloat16),
            pltpu.VMEM((rows, UNITS), jnp.float32),
            pltpu.VMEM((rows, UNITS), jnp.float32),
            by_unit,
            by_unit,
            by_unit,
            pltpu.SemaphoreType.DMA((2 * len(pieces),)),
            pltpu.SemaphoreType.DMA((3,)),
            pltpu.SemaphoreType.DMA((3 * -(-UNITS // TILE),)),
        ],
        compiler_params=pltpu.CompilerParams(vmem_limit_bytes=58 * 2**20),
        cost_estimate=pl.CostEstimate(
            flops=6 * rows * D * UNITS,
            bytes_accessed=6 * D * UNITS + 4 * rows * D + 6 * rows * UNITS,
            transcendentals=rows * UNITS,
        ),
    )(start, *sources, w_gate, w_up, w_down)


def grad_kernel(owners, sizes, offset_ref, scale_ref, *refs):
    groups, refs = refs[: 5 * len(sizes)], refs[5 * len(sizes) :]
    outs, (hidden, dgate, dup, left, right, wide, sems) = refs[:3], refs[3:]
    copies = {}
    for which, into in ((1, dgate), (2, dup), (0, hidden)):
        row = 0
        for at, size in enumerate(sizes):
            copy = pltpu.make_async_copy(
                groups[5 * at + which], into.at[pl.ds(row, size)], sems.at[3 * at + which]
            )
            copies[which, at] = copy
            row += size
            if which == 1:
                copy.start()
    row = 0
    for at in range(len(sizes)):
        inside = 0
        for owner, size in owners[at]:
            scale = scale_ref[owner]
            here, there = pl.ds(inside, size), pl.ds(row, size)
            for side, into in ((3, left), (4, right)):
                into[there, :] = (
                    groups[5 * at + side][here, :].astype(jnp.float32) * scale
                ).astype(jnp.bfloat16)
            inside += size
            row += size
    offset = pl.multiple_of(offset_ref[0], 32)
    place = 0
    for which, factor, array, out in (
        (1, left, dgate, outs[0]),
        (2, left, dup, outs[1]),
        (0, right, hidden, outs[2]),
    ):
        for at in range(len(sizes)):
            copies[which, at].wait()
        if which == 1:
            for later in (2, 0):
                for at in range(len(sizes)):
                    copies[later, at].start()
        for start in range(0, UNITS, TILE):
            tile = slice(start, min(start + TILE, UNITS))
            columns = slice(0, tile.stop - tile.start)
            wide[place % 3, :, columns] = contract_first(factor[...], array[:, tile])
            out[:, tile] = wide[place % 3, pl.ds(offset, SLICE), columns].astype(jnp.bfloat16)
            place += 1


def grad_work(offset, scales, groups, owners):
    sizes = [group[0].shape[0] for group in groups]
    rows = sum(sizes)
    far = pl.BlockSpec(memory_space=pl.ANY)
    vmem = pl.BlockSpec(memory_space=pltpu.VMEM)
    return pl.pallas_call(
        functools.partial(grad_kernel, owners, sizes),
        in_specs=[pl.BlockSpec(memory_space=pltpu.SMEM)] * 2
        + ([far] * 3 + [vmem] * 2) * len(sizes),
        out_shape=[jax.ShapeDtypeStruct((SLICE, UNITS), jnp.bfloat16)] * 3,
        scratch_shapes=[
            pltpu.VMEM((rows, UNITS), jnp.bfloat16),
            pltpu.VMEM((rows, UNITS), jnp.bfloat16),
            pltpu.VMEM((rows, UNITS), jnp.bfloat16),
            pltpu.VMEM((rows, WINDOW), jnp.bfloat16),
            pltpu.VMEM((rows, WINDOW), jnp.bfloat16),
            pltpu.VMEM((3, WINDOW, TILE), jnp.float32),
            pltpu.SemaphoreType.DMA((3 * len(sizes),)),
        ],
        compiler_params=pltpu.CompilerParams(vmem_limit_bytes=58 * 2**20),
        cost_estimate=pl.CostEstimate(
            flops=6 * rows * WINDOW * UNITS,
            bytes_accessed=6 * rows * UNITS + 6 * SLICE * UNITS + 4 * rows * WINDOW,
            transcendentals=0,
        ),
    )(offset, scales, *[array for group in groups for array in group])


def pick(array, index):
    return lax.dynamic_index_in_dim(array, index, 0, keepdims=False)


def after(arrays, *earlier):
    return lax.optimization_barrier((arrays, earlier))[0]


def mix_kernel(y_ref, core_ref, inputs, *refs):
    pieces, mixed, total = refs[:8], refs[8], refs[9]
    for side in range(2):
        for step in range(4):
            piece = pieces[4 * side + step]
            y_at = lax.rem(y_ref[0] + step, 4)
            core = core_ref[0] if side == 0 else 1 - core_ref[0]
            for x_high in range(2):
                row = (x_high * 8 + y_at * 2 + core) * OWN
                total[pl.ds(pl.multiple_of(row, 16), OWN), :] = piece[x_high, :OWN, :SEQ].astype(
                    jnp.float32
                )
    mixed[...] = (inputs[...].astype(jnp.float32) + total[...].T).astype(jnp.bfloat16)


def mix(y_at, core, inputs, pieces):
    smem = pl.BlockSpec(memory_space=pltpu.SMEM)
    vmem = pl.BlockSpec(memory_space=pltpu.VMEM)
    return pl.pallas_call(
        mix_kernel,
        in_specs=[smem, smem] + [vmem] * 9,
        out_shape=jax.ShapeDtypeStruct((SEQ, D), jnp.bfloat16),
        scratch_shapes=[pltpu.VMEM((D, SEQ), jnp.float32)],
        compiler_params=pltpu.CompilerParams(vmem_limit_bytes=24 * 2**20),
    )(y_at, core, inputs, *pieces)


def shards(inputs, norm_gain, w_gate, w_up, w_down, feat_dirs, unit_dirs, cotangent, lengths):
    t_index = lax.axis_index("tensor")
    d_index = lax.axis_index("dp")
    core = t_index % 2
    y_at = (t_index // 2) % 4
    x_high = t_index // 8
    core_index = core.astype(jnp.int32)[None]
    rows = inputs.reshape(SEQ, D)
    gain = norm_gain.reshape(D // 128, 128)
    normed, masked, mine, inverse = own_rows(
        core_index, lengths, rows, gain, cotangent.reshape(SEQ, D)
    )

    from_pair = move(mine, to_pair)
    from_down = move(mine, to_up)
    from_up = move(mine, to_down)

    first_column = d_index * SLICE
    window_start = (first_column // 128 * 128).astype(jnp.int32)[None]
    window_offset = (first_column % 128).astype(jnp.int32)[None]
    *own, kept, sent, own_normed_cut, own_cot_cut, own_cot = own_work(
        window_start, t_index.astype(jnp.int32)[None], normed, masked, rows, inverse,
        gain, w_gate, w_up, w_down, feat_dirs, unit_dirs,
    )
    own = (*own, own_normed_cut, own_cot_cut)

    from_pair, from_down, from_up, kept, sent = after(
        (from_pair, from_down, from_up, kept, sent), own
    )
    kept_sibling = move(sent, to_sibling)
    x_second = move(from_down, to_pair)
    up_second = move(from_down, to_up)
    first_sources = [(a, move(a, to_sibling)) for a in (from_pair, from_down, from_up)]
    kept = kept.astype(jnp.float32) + kept_sibling.astype(jnp.float32)
    kept = kept.astype(jnp.bfloat16).reshape(4, 2, ROWS, LANES)
    arrived = [move(pick(kept, (y_at + step) % 4), along_y(step)) for step in (2, 1, 3)]
    total = pick(kept, y_at)

    def group_of(sources, owners):
        pieces = []
        flat = []
        for at, (pair, owner) in enumerate(zip(sources, owners)):
            for which in range(2):
                for item in range(pair[0].shape[0]):
                    pieces.append((2 * at + which, item, 48))
                    flat.append((owner, 48))
        arrays = [a for pair in sources for a in pair]
        worked = unit_work(window_start, arrays, tuple(pieces), w_gate, w_up, w_down)
        return worked, tuple(flat)

    first_sources = after(first_sources, total)
    first, owners_first = group_of(first_sources, (1, 2, 4))

    arrived, total, x_second, up_second, from_pair = after(
        (arrived, total, x_second, up_second, from_pair), first
    )
    third = [move(from_pair, to_down), move(x_second, to_up)]
    second_sources = [(a, move(a, to_sibling)) for a in (x_second, up_second)]
    total = sum((a.astype(jnp.float32) for a in arrived), total.astype(jnp.float32))
    total = total.astype(jnp.bfloat16)
    total_far = move(total, to_far)

    second, owners_second = group_of(second_sources, (3, 6))

    total, total_far, third = after((total, total_far, third), second)
    third_sources = [(a, move(a, to_sibling)) for a in third]
    total = total.astype(jnp.float32) + total_far.astype(jnp.float32)
    loss_dot = total[:1, 2 * OWN, :K]
    bound = 0.5 * math.sqrt(SEQ * D * FF)
    own_ratio = jnp.sqrt(jnp.mean(loss_dot * loss_dot, axis=1)) / bound
    scale = 1.0 / (N_DP * jnp.maximum(own_ratio, 1.0))
    scale_row = jnp.broadcast_to(scale[None, :], (1, 128))
    scale_pair = move(scale_row, to_pair)
    branch = total[:, OWN:].astype(jnp.bfloat16)
    branches = [branch] + [move(branch, along_y(-step)) for step in (1, 2, 3)]

    third, owners_third = group_of(third_sources, (5, 7))

    scale_pair, branches = after((scale_pair, branches), third)
    two = jnp.concatenate([scale_row, scale_pair], axis=0)
    two_down = move(two, along_z(1))
    two_up = move(two, along_z(-1))
    two_far = move(two, along_z(2))
    siblings = [move(a, to_sibling) for a in branches]
    own_back = pick(total, x_high)[:OWN, :SEQ]
    grad_input = ((own_back + own_cot) * scale).astype(jnp.bfloat16).T.reshape(1, SEQ, OWN)

    scales = jnp.concatenate([two[:, 0], two_down[:, 0], two_up[:, 0], two_far[:, 0]])
    grads = grad_work(
        window_offset,
        scales,
        (own, first, second, third),
        (((0, SEQ),), owners_first, owners_second, owners_third),
    )
    branches, siblings = after((branches, siblings), grads)
    mixed = mix(
        y_at.astype(jnp.int32)[None], core_index, rows, branches + siblings
    ).reshape(1, SEQ, D)
    every_loss = jnp.stack([a[0, OWN, :K] for a in branches + siblings])
    shared_loss = pick(every_loss, (4 - y_at) % 4 + 4 * core).astype(jnp.float32)[None, :]
    norm_ratio = jnp.sqrt(jnp.mean(shared_loss * shared_loss, axis=1)) / bound
    return (mixed, norm_ratio, grad_input, grads[0], grads[1], grads[2].T)


def solution(mesh):
    placed = (
        P("dp", None, None),
        P(),
        P(None, "tensor"),
        P(None, "tensor"),
        P("tensor", None),
        P(),
        P(None, None, "tensor"),
        P("dp", None, None),
        P("dp"),
    )
    return jax.shard_map(
        shards,
        mesh=mesh,
        in_specs=placed,
        out_specs=(
            P("dp", None, None),
            P("dp"),
            P("dp", None, "tensor"),
            P("dp", "tensor"),
            P("dp", "tensor"),
            P("tensor", "dp"),
        ),
        check_vma=False,
    )
```
